256 devices in a mesh: group: 16 (over x, z_hi, core), rows: 16 (over z_lo, y).
Axes of the slice: x: 4, y: 4, z: 8 (z_hi: 2, z_lo: 4; z = z_hi * 4 + z_lo), core: 2. Of those that a mesh axis runs over, the one named last changes fastest.
Arguments:
- image: bfloat16 [2048, 128, 352], P(('group', 'rows')), parts along dimension 0, may hold values from -6 to 6
- visible: int32 [256, 16], P(('group', 'rows')), parts along dimension 0, may hold values 0 or 1
- layer_norm_gain: float32 [352], replicated, may hold values from 0.5 to 1.5
- reducer_weight: bfloat16 [1408, 704], replicated, may hold values from -0.15625 to 0.15625
- reducer_bias: float32 [704], replicated, may hold values from -3 to 3
- depth_kernel: float32 [49, 704], replicated, may hold values from -0.875 to 0.875
- depth_bias: float32 [704], replicated, may hold values from -3 to 3
- cotangent: bfloat16 [1024, 64, 704], P(('group', 'rows')), parts along dimension 0, may hold values from -6 to 6
Outputs:
- features: bfloat16 [1024, 64, 704], P(('group', 'rows')), parts along dimension 0
- image_grad: bfloat16 [2048, 128, 352], P(('group', 'rows')), parts along dimension 0
- down_weight_grad: float32 [22528, 704], P(('group', 'rows')), parts along dimension 0
- gain_grad: float32 [5632], P('group'), parts along dimension 0
- down_bias_grad: float32 [11264], P('group'), parts along dimension 0
- kernel_grad: float32 [784, 704], P('group'), parts along dimension 0
- depth_bias_grad: float32 [11264], P('group'), parts along dimension 0
The draws below stay inside these ranges and needn't reach their ends.
There are 16 independent parts, one for each index of `group`. The reference program is written for one: setup_inputs(seed, part) draws one part's arguments, and reference() takes and returns one part's arrays. A program takes and returns all parts, laid end to end along the dimension named above; an argument that names none is the same for every part. Nothing has to cross between parts.
Inputs may be any that keep to these rules, and one draw needn't show every extreme that they name: visible holds one 0 or 1 for each patch of 4 x 4 output pixels.
All inputs are finite; a program needn't handle non-finite values. No bound on the sum of `visible` on one device may be relied on, other than what follows from the above.
Results may differ from the reference program's by a relative error of at most 0.024.
Values may be sent and summed in bfloat16 or wider, within the bound.
No kernel may reach another device: no remote copies, remote signals or barrier semaphores. Data moves between devices by JAX's collectives and lax.ppermute only.
A program may use at most 64 MiB of HBM per device.

```python
import math
import jax
import jax.numpy as jnp
from jax import lax

C_IN = 352
C_OUT = 704
COLS = 64
KS = 7
PATCH = 4
H_OUT = 64


def with_ends(values, own_key, smallest, top_value):
    extent = values.shape
    spot = [jax.random.randint(jax.random.fold_in(own_key, axis), (), 0, extent[axis]) for axis in range(len(extent))]
    values = values.at[tuple(spot)].set(smallest)
    longest = extent.index(max(extent))
    spot[longest] = (spot[longest] + 1) % extent[longest]
    return values.at[tuple(spot)].set(top_value)


def block_levels(own_key, extent, cuts, least, top_value):
    level = 1.0
    for dim, parts in cuts:
        heights = jax.random.uniform(jax.random.fold_in(jax.random.fold_in(own_key, 6), dim), (parts,), jnp.float32, least / len(cuts), top_value / len(cuts))
        level = level * jnp.repeat(jnp.exp(heights), extent[dim] // parts).reshape((-1,) + (1,) * (len(extent) - 1 - dim))
    return level


def centred(own_key, extent, scale, reach, cuts=(), dtype=jnp.bfloat16):
    array = scale * jax.random.normal(own_key, extent, jnp.float32)
    if cuts:
        array = array * block_levels(own_key, extent, cuts, -0.22, 0.18)
    return jnp.clip(array, -reach, reach).astype(dtype)


def setup_inputs(seed: int = 0, part: int = 0) -> dict:
    seeds = jax.random.split(jax.random.key(seed), 9)
    part_keys = jax.random.split(jax.random.fold_in(seeds[8], part), 9)
    image = centred(part_keys[0], (2 * H_OUT, 2 * COLS, C_IN), 1.0, 6.0, ((0, 16),))
    visible = with_ends((jax.random.randint(part_keys[1], (H_OUT // PATCH, COLS // PATCH), 0, 5) < 2).astype(jnp.int32), jax.random.fold_in(part_keys[1], 1), 0, 1)
    layer_norm_gain = jnp.clip(1.0 + 0.1 * jax.random.normal(seeds[2], (C_IN,), jnp.float32), 0.5, 1.5)
    reducer_weight = centred(seeds[3], (4 * C_IN, C_OUT), (4 * C_IN) ** -0.5, 0.15625)
    reducer_bias = centred(seeds[4], (C_OUT,), 0.5, 3.0, (), jnp.float32)
    depth_kernel = centred(seeds[5], (KS * KS, C_OUT), (KS * KS) ** -0.5, 0.875, (), jnp.float32)
    depth_bias = centred(seeds[6], (C_OUT,), 0.5, 3.0, (), jnp.float32)
    cotangent = centred(part_keys[7], (H_OUT, COLS, C_OUT), 1.0, 6.0, ((0, 16),))
    return {"image": image, "visible": visible, "layer_norm_gain": layer_norm_gain, "reducer_weight": reducer_weight, "reducer_bias": reducer_bias, "depth_kernel": depth_kernel, "depth_bias": depth_bias, "cotangent": cotangent}


def standardize(image):
    xf = image.astype(jnp.float32)
    center = lax.optimization_barrier(jnp.mean(xf, axis=-1, keepdims=True))
    spread = lax.optimization_barrier(jnp.mean((xf - center) ** 2, axis=-1, keepdims=True))
    reciprocal_spread = 1.0 / jnp.sqrt(spread + 1e-06)
    return ((xf - center) * reciprocal_spread, reciprocal_spread)

def to_patches(scaled):
    height, width, chans = scaled.shape
    split = scaled.reshape(height // 2, 2, width // 2, 2, chans)
    return split.transpose(0, 2, 1, 3, 4).reshape(height // 2 * (width // 2), 4 * chans)

def from_patches(flat, height, width, chans):
    split = flat.reshape(height, width, 2, 2, chans)
    return split.transpose(0, 2, 1, 3, 4).reshape(2 * height, 2 * width, chans)

def reference(image, visible, layer_norm_gain, reducer_weight, reducer_bias, depth_kernel, depth_bias, cotangent):
    height, width, chans = cotangent.shape
    scale = 1.0 / math.sqrt(height * width)
    pixel_mask = jnp.repeat(jnp.repeat(visible, PATCH, 0), PATCH, 1).astype(jnp.float32)[:, :, None]
    normalized_input, reciprocal_spread = standardize(image)
    scaled = (normalized_input * layer_norm_gain).astype(jnp.bfloat16)
    patch_tiles = to_patches(scaled)
    pre = jnp.dot(patch_tiles, reducer_weight, preferred_element_type=jnp.float32) + reducer_bias
    reduce_step = (pre.reshape(height, width, chans) * pixel_mask).astype(jnp.bfloat16)
    padded = jnp.pad(reduce_step, ((3, 3), (3, 3), (0, 0)))
    acc = jnp.zeros((height, width, chans), jnp.float32)
    for i in range(KS):
        for j in range(KS):
            acc = acc + padded[i:i + height, j:j + width].astype(jnp.float32) * depth_kernel[KS * i + j]
    depth = pixel_mask * (acc + depth_bias)
    features = (reduce_step.astype(jnp.float32) + depth).astype(jnp.bfloat16)
    masked_cot = (pixel_mask * cotangent.astype(jnp.float32)).astype(jnp.bfloat16)
    cot_pad = jnp.pad(masked_cot, ((3, 3), (3, 3), (0, 0)))
    back = jnp.zeros((height, width, chans), jnp.float32)
    kernel_terms = []
    masked_f = masked_cot.astype(jnp.float32)
    for i in range(KS):
        for j in range(KS):
            back = back + cot_pad[6 - i:6 - i + height, 6 - j:6 - j + width].astype(jnp.float32) * depth_kernel[KS * i + j]
            kernel_terms.append(lax.optimization_barrier(jnp.sum(padded[i:i + height, j:j + width].astype(jnp.float32) * masked_f, axis=(0, 1))))
    kernel_grad = jnp.stack(kernel_terms) * scale
    depth_bias_grad = lax.optimization_barrier(jnp.sum(masked_f, axis=(0, 1))) * scale
    down_cot = cotangent.astype(jnp.float32) + back
    pre_cot = (pixel_mask * down_cot).astype(jnp.bfloat16).reshape(height * width, chans)
    down_weight_grad = jnp.dot(patch_tiles.T, pre_cot, preferred_element_type=jnp.float32) * scale
    down_bias_grad = lax.optimization_barrier(jnp.sum(pre_cot.astype(jnp.float32), axis=0)) * scale
    flat_cot = jnp.dot(pre_cot, reducer_weight.T, preferred_element_type=jnp.float32)
    scaled_cot = from_patches(flat_cot, height, width, image.shape[2])
    gain_grad = lax.optimization_barrier(jnp.sum(normalized_input * scaled_cot, axis=(0, 1))) * scale
    gathered = scaled_cot * layer_norm_gain
    image_grad = reciprocal_spread * (gathered - lax.optimization_barrier(jnp.mean(gathered, axis=-1, keepdims=True)) - normalized_input * lax.optimization_barrier(jnp.mean(gathered * normalized_input, axis=-1, keepdims=True)))
    return (features, image_grad.astype(jnp.bfloat16), down_weight_grad, gain_grad, down_bias_grad, kernel_grad, depth_bias_grad)
```

```python
import math

import jax
import jax.numpy as jnp
from jax import lax
from jax.experimental import pallas as pl
from jax.experimental.pallas import tpu as pltpu
from jax.sharding import PartitionSpec as P

KS = 7
PATCH = 4
LANES = 128
F32 = jnp.float32
BF16 = jnp.bfloat16
VM = pl.BlockSpec(memory_space=pltpu.VMEM)
SM = pl.BlockSpec(memory_space=pltpu.SMEM)


def tiles_of(chans):
    return [(t, min(LANES, chans - t * LANES)) for t in range(-(-chans // LANES))]


def column_mask(vis_ref, width):
    row = lax.broadcasted_iota(jnp.int32, (width, LANES), 0) // PATCH
    mask = jnp.zeros((width, LANES), F32)
    for k in range(width // PATCH):
        mask = jnp.where(row == k, vis_ref[0, k].astype(F32), mask)
    return mask


def call(kernel, out_shape, in_specs, scratch, flops, size, name):
    return pl.pallas_call(
        kernel,
        out_shape=out_shape,
        in_specs=in_specs,
        out_specs=jax.tree.map(lambda _: VM, out_shape),
        scratch_shapes=scratch,
        compiler_params=pltpu.CompilerParams(vmem_limit_bytes=48 * 2**20),
        cost_estimate=pl.CostEstimate(flops=flops, bytes_accessed=size, transcendentals=0),
        name=name,
    )


def edge_kernel(vis, cot, first, last):
    height, width, chans = cot.shape
    mask = column_mask(vis, width)
    for t, wd in tiles_of(chans):
        lanes = slice(t * LANES, t * LANES + wd)
        for p in range(height):
            row = (cot[p, :, lanes].astype(F32) * mask[:, :wd]).astype(BF16)
            if p < 3:
                first[p, :, lanes] = row
            if p >= height - 3:
                last[p - (height - 3), :, lanes] = row


def reduce_kernel(vis, image, gain, weight, bias, patches, normed, rstd, down, first, last, spread):
    rows, cols, chans = image.shape
    height, width = rows // 2, cols // 2
    mask = column_mask(vis, width)
    wide = tiles_of(chans)
    for r in range(rows):
        p, a = r // 2, r % 2
        x = image[r].astype(F32)
        center = jnp.sum(x, axis=-1, keepdims=True) * (1.0 / chans)
        x = x - center
        var = jnp.sum(x * x, axis=-1, keepdims=True) * (1.0 / chans)
        inv = 1.0 / jnp.sqrt(var + 1e-06)
        x = x * inv
        for t, wd in wide:
            spread[r, t, :, 0:wd] = x[:, t * LANES : t * LANES + wd]
        spread[r, len(wide)] = jnp.broadcast_to(inv, (cols, LANES))
        for b in range(2):
            at = pl.ds(p * width, width)
            for t, wd in wide:
                lanes = slice(t * LANES, t * LANES + wd)
                part = spread[r, t, pl.ds(b, width, stride=2), :][:, :wd]
                normed[2 * a + b, at, lanes] = part.astype(BF16)
                patches[2 * a + b, at, lanes] = (part * gain[:, lanes]).astype(BF16)
            rstd[2 * a + b, at, :] = spread[r, len(wide), pl.ds(b, width, stride=2), :]
    acc = jnp.zeros((height * width, weight.shape[1]), F32)
    for k in range(4):
        acc = acc + jnp.dot(
            patches[k], weight[k * chans : (k + 1) * chans, :], preferred_element_type=F32
        )
    acc = acc + bias[...]
    for t, wd in tiles_of(weight.shape[1]):
        lanes = slice(t * LANES, t * LANES + wd)
        for p in range(height):
            row = (acc[p * width : (p + 1) * width, lanes] * mask[:, :wd]).astype(BF16)
            down[p, :, lanes] = row
            if p < 3:
                first[p, :, lanes] = row
            if p >= height - 3:
                last[p - (height - 3), :, lanes] = row


def fill_band(dst, before, own, after, scale):
    count, width, chans = own.shape
    parts = [(before, k) for k in range(3)] + [(own, k) for k in range(count)]
    parts += [(after, k) for k in range(3)]
    tiles = tiles_of(chans)
    edge = jnp.zeros((len(tiles), len(parts), 8, LANES), F32)
    dst[:, :, 0:8, :] = edge
    dst[:, :, 8 + width : 16 + width, :] = edge
    for t, wd in tiles:
        if wd < LANES:
            dst[t, :, 8 : 8 + width, wd:LANES] = jnp.zeros((len(parts), width, LANES - wd), F32)
        for k, (ref, at) in enumerate(parts):
            value = ref[at, :, t * LANES : t * LANES + wd].astype(F32)
            if scale is not None and ref is own:
                value = value * scale[:, :wd]
            dst[t, k, 8 : 8 + width, 0:wd] = value


def fill_taps(dst, kernel):
    taps, chans = kernel.shape
    for t, wd in tiles_of(chans):
        dst[t, :, :, 0:wd] = jnp.broadcast_to(
            kernel[:, t * LANES : t * LANES + wd][:, None, :], (taps, 8, wd)
        )
        if wd < LANES:
            dst[t, :, :, wd:LANES] = jnp.zeros((taps, 8, LANES - wd), F32)


def back_kernel(place, vis, cot, before, after, kernel, patches, pre, *rest):
    chunks, (band, taps, mask_s, total, prod) = rest[:4], rest[4:]
    height, width, chans = cot.shape
    mask = column_mask(vis, width)
    mask_s[...] = mask
    fill_band(band, before, cot, after, mask)
    fill_taps(taps, kernel)
    half = width // 2
    groups = half // 8

    def step(u, carry):
        t, h = u // 2, (u % 2) * half
        acc = [jnp.zeros((groups, 8, LANES), F32) for _ in range(height)]
        for s in range(height + 6):
            for j in range(KS):
                value = band[t, s, pl.ds(h + 5 + j, half), :].reshape(groups, 8, LANES)
                for p in range(height):
                    i = s - p
                    if 0 <= i < KS:
                        acc[p] = acc[p] + value * taps[t, 48 - (KS * i + j)][None]
        here = pl.ds(pl.multiple_of(h, 8), half)
        keep = mask_s[here, :]
        lanes = pl.ds(pl.multiple_of(t * LANES, LANES), LANES)
        for p in range(height):
            own = band[t, 3 + p, pl.ds(pl.multiple_of(h + 8, 8), half), :]
            value = own + keep * acc[p].reshape(half, LANES)
            total[pl.ds(pl.multiple_of(p * width + h, 8), half), lanes] = value
        return carry

    lax.fori_loop(0, 2 * len(tiles_of(chans)), step, 0)
    pre[...] = total[:, :chans].astype(BF16)
    scale = 1.0 / math.sqrt(height * 16 * width)
    share = patches.shape[2] // 4
    for k in range(4):
        prod[...] = (
            lax.dot_general(
                patches[k], pre[...], (((0,), (0,)), ((), ())), preferred_element_type=F32
            )
            * scale
        )
        for d in range(4):
            to = lax.rem(place[0] + d, 4)
            at = pl.ds(pl.multiple_of(to * share, 8), share)
            chunks[d][k] = prod[at, :].astype(BF16)


def front_kernel(vis, down, before, after, kernel, bias, cot, features, grads, band, taps, cots, outs, kg):
    height, width, chans = cot.shape
    mask = column_mask(vis, width)
    fill_band(band, before, down, after, None)
    fill_taps(taps, kernel)
    for t, wd in tiles_of(chans):
        if wd < LANES:
            cots[t, :, :, wd:LANES] = jnp.zeros((height, width, LANES - wd), F32)
        for p in range(height):
            value = cot[p, :, t * LANES : t * LANES + wd].astype(F32)
            cots[t, p, :, 0:wd] = value * mask[:, :wd]
    half = width // 2
    groups = half // 8

    def step(u, carry):
        t, h = u // 2, (u % 2) * half
        here = pl.ds(pl.multiple_of(h, 8), half)
        acc = [jnp.zeros((groups, 8, LANES), F32) for _ in range(height)]
        mine = [cots[t, p, here, :].reshape(groups, 8, LANES) for p in range(height)]
        for j in range(KS):
            part = [jnp.zeros((8, LANES), F32) for _ in range(KS)]
            for s in range(height + 6):
                value = band[t, s, pl.ds(h + 5 + j, half), :].reshape(groups, 8, LANES)
                for p in range(height):
                    i = s - p
                    if 0 <= i < KS:
                        acc[p] = acc[p] + value * taps[t, KS * i + j][None]
                        part[i] = part[i] + jnp.sum(value * mine[p], axis=0)
            for i in range(KS):
                kg[u, KS * i + j] = part[i]
        kg[u, KS * KS] = sum(jnp.sum(m, axis=0) for m in mine)
        for p in range(height):
            outs[t, p, here, :] = acc[p].reshape(half, LANES)
        return carry

    tiles = tiles_of(chans)
    lax.fori_loop(0, 2 * len(tiles), step, 0)
    scale = 1.0 / math.sqrt(height * 16 * width)
    for t, wd in tiles:
        lanes = slice(t * LANES, t * LANES + wd)
        for p in range(height):
            value = (outs[t, p, :, 0:wd] + bias[:, lanes]) * mask[:, :wd]
            own = band[t, 3 + p, 8 : 8 + width, 0:wd]
            features[p, :, lanes] = (own + value).astype(BF16)
        term = jnp.sum(kg[2 * t] + kg[2 * t + 1], axis=1) * scale
        grads[0 : KS * KS + 1, lanes] = term[:, :wd]


def image_kernel(pre, weight, normed, rstd, gain, grads, image_grad, small, spread, sums):
    rows, cols, chans = image_grad.shape
    height, width = rows // 2, cols // 2
    wide = tiles_of(chans)
    scale = 1.0 / math.sqrt(height * 16 * width)
    gain_sum = jnp.zeros((1, chans), F32)
    for k in range(4):
        a, b = k // 2, k % 2
        flat = lax.dot_general(
            pre[...],
            weight[k * chans : (k + 1) * chans, :],
            (((1,), (1,)), ((), ())),
            preferred_element_type=F32,
        )
        norm = normed[k].astype(F32)
        gain_sum = gain_sum + jnp.sum(norm * flat, axis=0, keepdims=True)
        g = flat * gain[...]
        mean_g = jnp.sum(g, axis=-1, keepdims=True) * (1.0 / chans)
        mean_n = jnp.sum(g * norm, axis=-1, keepdims=True) * (1.0 / chans)
        g = g - mean_g - norm * mean_n
        for t, wd in wide:
            part = g[:, t * LANES : t * LANES + wd] * rstd[k][:, :wd]
            for p in range(height):
                spread[2 * p + a, t, pl.ds(b, width, stride=2), 0:wd] = part[
                    p * width : (p + 1) * width
                ]
    for r in range(rows):
        for t, wd in wide:
            image_grad[r, :, t * LANES : t * LANES + wd] = spread[r, t, :, 0:wd].astype(BF16)
    bias_sum = jnp.sum(pre[...].astype(F32), axis=0, keepdims=True)
    taps = KS * KS + 1
    sums[...] = jnp.zeros(sums.shape, F32)
    sums[0:taps, :] = grads[0:taps, :]
    sums[taps : taps + 1, :] = bias_sum * scale
    sums[taps + 1 : taps + 2, 0:chans] = gain_sum * scale
    small[...] = sums[...].astype(BF16)


def sd(shape, dtype):
    return jax.ShapeDtypeStruct(shape, dtype)


def sum_four(own, one, two, three):
    return (own.astype(F32) + two.astype(F32)) + (one.astype(F32) + three.astype(F32))


def body(image, visible, layer_norm_gain, reducer_weight, reducer_bias, depth_kernel, depth_bias, cotangent):
    height, width, chans = cotangent.shape
    rows, cols, in_chans = image.shape
    pixels = height * width
    bands = lax.axis_size("rows")
    index = lax.axis_index("rows")
    place_y, place_z = index % 4, index // 4
    up = [(i, i + 1) for i in range(bands - 1)]
    down_perm = [(j, i) for i, j in up]
    along_y = [[(4 * z + y, 4 * z + (y + k) % 4) for z in range(4) for y in range(4)] for k in range(4)]
    along_z = [[(4 * z + y, 4 * ((z + k) % 4) + y) for z in range(4) for y in range(4)] for k in range(4)]
    tiles = len(tiles_of(chans))
    in_tiles = len(tiles_of(in_chans))
    halo = sd((3, width, chans), BF16)
    macs = pixels * chans * 4 * in_chans
    taps = pixels * chans * KS * KS
    gain = layer_norm_gain.reshape(1, in_chans)

    cot_first, cot_last = call(
        edge_kernel, (halo, halo), [SM, VM], [], pixels * chans, 10**6, "edge"
    )(visible, cotangent)
    cot_before = lax.ppermute(cot_last, "rows", up)
    cot_after = lax.ppermute(cot_first, "rows", down_perm)

    patches, normed, rstd, down, first, last = call(
        reduce_kernel,
        (
            sd((4, pixels, in_chans), BF16),
            sd((4, pixels, in_chans), BF16),
            sd((4, pixels, LANES), F32),
            sd((height, width, chans), BF16),
            halo,
            halo,
        ),
        [SM, VM, VM, VM, VM],
        [pltpu.VMEM((rows, in_tiles + 1, cols, LANES), F32)],
        2 * macs,
        8 * 10**6,
        "reduce",
    )(visible, image, gain, reducer_weight, reducer_bias.reshape(1, chans))
    down_before = lax.ppermute(last, "rows", up)
    down_after = lax.ppermute(first, "rows", down_perm)

    share = in_chans // 4
    band = pltpu.VMEM((tiles, height + 6, width + 16, LANES), F32)
    taps_s = pltpu.VMEM((tiles, KS * KS, 8, LANES), F32)
    pre, *chunks = call(
        back_kernel,
        (sd((pixels, chans), BF16),) + (sd((4, share, chans), BF16),) * 4,
        [SM, SM, VM, VM, VM, VM, VM],
        [
            band,
            taps_s,
            pltpu.VMEM((width, LANES), F32),
            pltpu.VMEM((pixels, tiles * LANES), F32),
            pltpu.VMEM((in_chans, chans), F32),
        ],
        2 * macs + 40 * taps,
        6 * 10**6,
        "back",
    )(place_y.reshape(1).astype(jnp.int32), visible, cotangent, cot_before, cot_after, depth_kernel, patches)

    got = [lax.ppermute(chunks[k], "rows", along_y[k]) for k in (1, 2, 3)]

    features, grads = call(
        front_kernel,
        (sd((height, width, chans), BF16), sd((56, chans), F32)),
        [SM, VM, VM, VM, VM, VM, VM],
        [
            band,
            taps_s,
            pltpu.VMEM((tiles, height, width, LANES), F32),
            pltpu.VMEM((tiles, height, width, LANES), F32),
            pltpu.VMEM((2 * tiles, KS * KS + 1, 8, LANES), F32),
        ],
        80 * taps,
        6 * 10**6,
        "front",
    )(visible, down, down_before, down_after, depth_kernel, depth_bias.reshape(1, chans), cotangent)

    image_grad, small = call(
        image_kernel,
        (sd((rows, cols, in_chans), BF16), sd((64, chans), BF16)),
        [VM] * 6,
        [pltpu.VMEM((rows, in_tiles, cols, LANES), F32), pltpu.VMEM((64, chans), F32)],
        2 * macs,
        8 * 10**6,
        "image",
    )(pre, reducer_weight, normed, rstd, gain, grads)

    tiny = [lax.ppermute(small, "rows", along_y[k]) for k in (1, 2, 3)]
    small = sum_four(small, *tiny).astype(BF16)

    half = sum_four(chunks[0], *got).astype(BF16)
    parts = [lax.dynamic_index_in_dim(half, (place_z + k) % 4, 0, False) for k in range(4)]
    got = [lax.ppermute(parts[k], "rows", along_z[k]) for k in (1, 2, 3)]
    tiny = [lax.ppermute(small, "rows", along_z[k]) for k in (1, 2, 3)]
    down_weight_grad = sum_four(parts[0], *got)
    small = sum_four(small, *tiny)
    n = KS * KS
    return (
        features,
        image_grad,
        down_weight_grad,
        small[n + 2, :in_chans],
        small[n + 1],
        small[:n],
        small[n],
    )


def solution(mesh):
    placed = (
        P(("group", "rows"), None, None),
        P(("group", "rows"), None),
        P(),
        P(),
        P(),
        P(),
        P(),
        P(("group", "rows"), None, None),
    )
    return jax.shard_map(
        body,
        mesh=mesh,
        in_specs=placed,
        out_specs=(
            P(("group", "rows"), None, None),
            P(("group", "rows"), None, None),
            P(("group", "rows"), None),
            P("group"),
            P("group"),
            P("group", None),
            P("group"),
        ),
        check_vma=False,
    )
```

```python
import math

import jax
import jax.numpy as jnp
from jax import lax
from jax.experimental import pallas as pl
from jax.experimental.pallas import tpu as pltpu
from jax.sharding import PartitionSpec as P

KS = 7
PATCH = 4
LANES = 128
F32 = jnp.float32
BF16 = jnp.bfloat16
VM = pl.BlockSpec(memory_space=pltpu.VMEM)
SM = pl.BlockSpec(memory_space=pltpu.SMEM)
ANY = pl.BlockSpec(memory_space=pl.ANY)


def tiles_of(chans):
    return [(t, min(LANES, chans - t * LANES)) for t in range(-(-chans // LANES))]


def column_mask(vis_ref, width):
    row = lax.broadcasted_iota(jnp.int32, (width, LANES), 0) // PATCH
    mask = jnp.zeros((width, LANES), F32)
    for k in range(width // PATCH):
        mask = jnp.where(row == k, vis_ref[0, k].astype(F32), mask)
    return mask


def call(kernel, out_shape, in_specs, scratch, flops, size, name):
    return pl.pallas_call(
        kernel,
        out_shape=out_shape,
        in_specs=in_specs,
        out_specs=jax.tree.map(lambda _: VM, out_shape),
        scratch_shapes=scratch,
        compiler_params=pltpu.CompilerParams(vmem_limit_bytes=20 * 2**20),
        cost_estimate=pl.CostEstimate(flops=flops, bytes_accessed=size, transcendentals=0),
        name=name,
    )


def edge_kernel(vis, cot, first, last):
    height, width, chans = cot.shape
    mask = column_mask(vis, width)
    for t, wd in tiles_of(chans):
        lanes = slice(t * LANES, t * LANES + wd)
        for p in range(height):
            row = (cot[p, :, lanes].astype(F32) * mask[:, :wd]).astype(BF16)
            if p < 3:
                first[p, :, lanes] = row
            if p >= height - 3:
                last[p - (height - 3), :, lanes] = row


def sorter(width, back):
    size = 4 * width
    row = lax.broadcasted_iota(jnp.int32, (size, size), 1 if back else 0)
    col = lax.broadcasted_iota(jnp.int32, (size, size), 0 if back else 1)
    half, rest = col // (2 * width), col % (2 * width)
    source = (rest // width) * (2 * width) + 2 * (rest % width) + half
    return jnp.where(row == source, 1.0, 0.0).astype(BF16)


def gain_column(gain, column):
    column[...] = jnp.transpose(jnp.broadcast_to(gain[...][None], (LANES, gain.shape[0])))


def reduce_kernel(
    vis, image, gain, weight, bias, order, patches, normed, rstd, down, first, last, column, sort
):
    rows, chans, cols = image.shape
    height, width = rows // 2, cols // 2
    mask = column_mask(vis, width)
    gain_column(gain, column)
    sort[...] = sorter(width, False)
    for a in range(2):
        for pair in range(height // 2):
            top = 4 * pair + a
            two = jnp.concatenate([image[top], image[top + 2]], axis=1)
            x = jnp.dot(two, sort[...], preferred_element_type=F32)
            center = jnp.sum(x, axis=0, keepdims=True) * (1.0 / chans)
            x = x - center
            var = jnp.sum(x * x, axis=0, keepdims=True) * (1.0 / chans)
            inv = 1.0 / jnp.sqrt(var + 1e-06)
            x = x * inv
            lanes = slice(pair * LANES, (pair + 1) * LANES)
            for b in range(2):
                k = 2 * a + b
                here = slice(k * chans, (k + 1) * chans)
                part = x[:, b * LANES : (b + 1) * LANES]
                normed[here, lanes] = part.astype(BF16)
                patches[here, lanes] = (part * column[...]).astype(BF16)
                rstd[k : k + 1, lanes] = inv[:, b * LANES : (b + 1) * LANES]
    acc = jnp.dot(weight[...], patches[...], preferred_element_type=F32)
    acc = jnp.transpose(acc) + bias[...][None]
    for t, wd in tiles_of(weight.shape[0]):
        lanes = slice(t * LANES, t * LANES + wd)
        for p in range(height):
            row = (acc[p * width : (p + 1) * width, lanes] * mask[:, :wd]).astype(BF16)
            down[p, :, lanes] = row
            if p < 3:
                first[p, :, lanes] = row
            if p >= height - 3:
                last[p - (height - 3), :, lanes] = row


def fill_band(dst, before, own, after, scale):
    count, width, chans = own.shape
    parts = [(before, k) for k in range(3)] + [(own, k) for k in range(count)]
    parts += [(after, k) for k in range(3)]
    tiles = tiles_of(chans)
    edge = jnp.zeros((len(tiles), len(parts), 8, LANES), F32)
    dst[:, :, 0:8, :] = edge
    dst[:, :, 8 + width : 16 + width, :] = edge
    for t, wd in tiles:
        if wd < LANES:
            dst[t, :, 8 : 8 + width, wd:LANES] = jnp.zeros((len(parts), width, LANES - wd), F32)
        for k, (ref, at) in enumerate(parts):
            value = ref[at, :, t * LANES : t * LANES + wd].astype(F32)
            if scale is not None and ref is own:
                value = value * scale[:, :wd]
            dst[t, k, 8 : 8 + width, 0:wd] = value


def fill_taps(dst, kernel):
    taps, chans = kernel.shape
    for t, wd in tiles_of(chans):
        dst[t, :, :, 0:wd] = jnp.broadcast_to(
            kernel[:, t * LANES : t * LANES + wd][:, None, :], (taps, 8, wd)
        )
        if wd < LANES:
            dst[t, :, :, wd:LANES] = jnp.zeros((taps, 8, LANES - wd), F32)


def back_kernel(place, vis, cot, before, after, kernel, patches, pre, *rest):
    chunks, (band, taps, mask_s, total, prod) = rest[:4], rest[4:]
    height, width, chans = cot.shape
    mask = column_mask(vis, width)
    mask_s[...] = mask
    fill_band(band, before, cot, after, mask)
    fill_taps(taps, kernel)
    half = width // 2
    groups = half // 8

    def step(u, carry):
        t, h = u // 2, (u % 2) * half
        acc = [jnp.zeros((groups, 8, LANES), F32) for _ in range(height)]
        for s in range(height + 6):
            for j in range(KS):
                value = band[t, s, pl.ds(h + 5 + j, half), :].reshape(groups, 8, LANES)
                for p in range(height):
                    i = s - p
                    if 0 <= i < KS:
                        acc[p] = acc[p] + value * taps[t, 48 - (KS * i + j)][None]
        here = pl.ds(pl.multiple_of(h, 8), half)
        keep = mask_s[here, :]
        lanes = pl.ds(pl.multiple_of(t * LANES, LANES), LANES)
        for p in range(height):
            own = band[t, 3 + p, pl.ds(pl.multiple_of(h + 8, 8), half), :]
            value = own + keep * acc[p].reshape(half, LANES)
            total[pl.ds(pl.multiple_of(p * width + h, 8), half), lanes] = value
        return carry

    lax.fori_loop(0, 2 * len(tiles_of(chans)), step, 0)
    pre[...] = total[:, :chans].astype(BF16)
    scale = 1.0 / math.sqrt(height * 16 * width)
    depth = patches.shape[0] // 4
    share = depth // 4
    for k in range(4):
        prod[...] = scale * jnp.dot(
            patches[k * depth : (k + 1) * depth, :], pre[...], preferred_element_type=F32
        )
        for d in range(4):
            to = lax.rem(place[0] + d, 4)
            at = pl.ds(pl.multiple_of(to * share, 8), share)
            chunks[d][k] = prod[at, :].astype(BF16)


def front_kernel(
    vis, down, before, after, kernel, bias, cot, order, features, grads, band, taps, cots, outs, kg
):
    height, width, chans = cot.shape
    mask = column_mask(vis, width)
    fill_band(band, before, down, after, None)
    fill_taps(taps, kernel)
    for t, wd in tiles_of(chans):
        if wd < LANES:
            cots[t, :, :, wd:LANES] = jnp.zeros((height, width, LANES - wd), F32)
        for p in range(height):
            value = cot[p, :, t * LANES : t * LANES + wd].astype(F32)
            cots[t, p, :, 0:wd] = value * mask[:, :wd]
    half = width // 2
    groups = half // 8

    def step(u, carry):
        t, h = u // 2, (u % 2) * half
        here = pl.ds(pl.multiple_of(h, 8), half)
        acc = [jnp.zeros((groups, 8, LANES), F32) for _ in range(height)]
        mine = [cots[t, p, here, :].reshape(groups, 8, LANES) for p in range(height)]
        for j in range(KS):
            part = [jnp.zeros((8, LANES), F32) for _ in range(KS)]
            for s in range(height + 6):
                value = band[t, s, pl.ds(h + 5 + j, half), :].reshape(groups, 8, LANES)
                for p in range(height):
                    i = s - p
                    if 0 <= i < KS:
                        acc[p] = acc[p] + value * taps[t, KS * i + j][None]
                        part[i] = part[i] + jnp.sum(value * mine[p], axis=0)
            for i in range(KS):
                kg[u, KS * i + j] = part[i]
        kg[u, KS * KS] = sum(jnp.sum(m, axis=0) for m in mine)
        for p in range(height):
            outs[t, p, here, :] = acc[p].reshape(half, LANES)
        return carry

    tiles = tiles_of(chans)
    lax.fori_loop(0, 2 * len(tiles), step, 0)
    scale = 1.0 / math.sqrt(height * 16 * width)
    for t, wd in tiles:
        lanes = slice(t * LANES, t * LANES + wd)
        for p in range(height):
            value = (outs[t, p, :, 0:wd] + bias[lanes][None]) * mask[:, :wd]
            own = band[t, 3 + p, 8 : 8 + width, 0:wd]
            features[p, :, lanes] = (own + value).astype(BF16)
        term = jnp.sum(kg[2 * t] + kg[2 * t + 1], axis=1) * scale
        grads[0 : KS * KS + 1, lanes] = term[:, :wd]


def image_kernel(
    pre, weight, normed, rstd, gain, grads, image_grad, small, column, sort, flat, sums
):
    rows, chans, cols = image_grad.shape
    height, width = rows // 2, cols // 2
    scale = 1.0 / math.sqrt(height * 16 * width)
    gain_column(gain, column)
    sort[...] = sorter(width, True)
    flat[...] = jnp.transpose(jnp.dot(pre[...], weight[...], preferred_element_type=F32))
    gain_sum = jnp.zeros((chans, LANES), F32)
    for a in range(2):
        for pair in range(height // 2):
            top = 4 * pair + a
            lanes = slice(pair * LANES, (pair + 1) * LANES)
            two = []
            for b in range(2):
                k = 2 * a + b
                here = slice(k * chans, (k + 1) * chans)
                value = flat[here, lanes]
                norm = normed[here, lanes].astype(F32)
                gain_sum = gain_sum + norm * value
                g = value * column[...]
                mean_g = jnp.sum(g, axis=0, keepdims=True) * (1.0 / chans)
                mean_n = jnp.sum(g * norm, axis=0, keepdims=True) * (1.0 / chans)
                g = (g - mean_g - norm * mean_n) * rstd[k : k + 1, lanes]
                two.append(g.astype(BF16))
            out = jnp.dot(jnp.concatenate(two, axis=1), sort[...], preferred_element_type=F32)
            image_grad[top] = out[:, :cols].astype(BF16)
            image_grad[top + 2] = out[:, cols:].astype(BF16)
    ones = jnp.ones((8, pre.shape[0]), BF16)
    bias_sum = jnp.dot(ones, pre[...], preferred_element_type=F32)[0:1]
    gain_row = jnp.sum(jnp.transpose(gain_sum), axis=0, keepdims=True)
    taps = KS * KS + 1
    sums[...] = jnp.zeros(sums.shape, F32)
    sums[0:taps, :] = grads[0:taps, :]
    sums[taps : taps + 1, :] = bias_sum * scale
    sums[taps + 1 : taps + 2, 0:chans] = gain_row * scale
    small[...] = sums[...].astype(BF16)


def last_kernel(w0, w1, w2, w3, t0, t1, t2, t3, weight, gain, bias, kernel, depth_bias):
    weight[...] = sum_four(w0[...], w1[...], w2[...], w3[...])
    total = sum_four(t0[...], t1[...], t2[...], t3[...])
    taps = KS * KS
    kernel[...] = total[:taps]
    depth_bias[...] = total[taps]
    bias[...] = total[taps + 1]
    gain[...] = total[taps + 2, : gain.shape[0]]


def sd(shape, dtype):
    return jax.ShapeDtypeStruct(shape, dtype)


def sum_four(own, one, two, three):
    return (own.astype(F32) + two.astype(F32)) + (one.astype(F32) + three.astype(F32))


def body(image, visible, layer_norm_gain, reducer_weight, reducer_bias, depth_kernel, depth_bias, cotangent):
    height, width, chans = cotangent.shape
    rows, cols, in_chans = image.shape
    image = jnp.transpose(image, (0, 2, 1))
    weight = jnp.transpose(reducer_weight)
    pixels = height * width
    bands = lax.axis_size("rows")
    index = lax.axis_index("rows")
    place_y, place_z = index % 4, index // 4
    up = [(i, i + 1) for i in range(bands - 1)]
    down_perm = [(j, i) for i, j in up]
    along_y = [[(4 * z + y, 4 * z + (y + k) % 4) for z in range(4) for y in range(4)] for k in range(4)]
    along_z = [[(4 * z + y, 4 * ((z + k) % 4) + y) for z in range(4) for y in range(4)] for k in range(4)]
    tiles = len(tiles_of(chans))
    in_tiles = len(tiles_of(in_chans))
    halo = sd((3, width, chans), BF16)
    macs = pixels * chans * 4 * in_chans
    taps = pixels * chans * KS * KS
    gain = layer_norm_gain

    cot_first, cot_last = call(
        edge_kernel, (halo, halo), [SM, VM], [], pixels * chans, 10**6, "edge"
    )(visible, cotangent)
    cot_before = lax.ppermute(cot_last, "rows", up)
    cot_after = lax.ppermute(cot_first, "rows", down_perm)

    column = pltpu.VMEM((in_chans, LANES), F32)
    sort = pltpu.VMEM((4 * width, 4 * width), BF16)
    patches, normed, rstd, down, first, last = call(
        reduce_kernel,
        (
            sd((4 * in_chans, pixels), BF16),
            sd((4 * in_chans, pixels), BF16),
            sd((8, pixels), F32),
            sd((height, width, chans), BF16),
            halo,
            halo,
        ),
        [SM, VM, VM, VM, VM, ANY],
        [column, sort],
        2 * macs,
        8 * 10**6,
        "reduce",
    )(visible, image, gain, weight, reducer_bias, cot_first)
    down_before = lax.ppermute(last, "rows", up)
    down_after = lax.ppermute(first, "rows", down_perm)

    share = in_chans // 4
    band = pltpu.VMEM((tiles, height + 6, width + 16, LANES), F32)
    taps_s = pltpu.VMEM((tiles, KS * KS, 8, LANES), F32)
    pre, *chunks = call(
        back_kernel,
        (sd((pixels, chans), BF16),) + (sd((4, share, chans), BF16),) * 4,
        [SM, SM, VM, VM, VM, VM, VM],
        [
            band,
            taps_s,
            pltpu.VMEM((width, LANES), F32),
            pltpu.VMEM((pixels, tiles * LANES), F32),
            pltpu.VMEM((in_chans, chans), F32),
        ],
        2 * macs + 40 * taps,
        6 * 10**6,
        "back",
    )(place_y.reshape(1).astype(jnp.int32), visible, cotangent, cot_before, cot_after, depth_kernel, patches)

    got = [lax.ppermute(chunks[k], "rows", along_y[k]) for k in (1, 2, 3)]

    features, grads = call(
        front_kernel,
        (sd((height, width, chans), BF16), sd((56, chans), F32)),
        [SM, VM, VM, VM, VM, VM, VM, ANY],
        [
            band,
            taps_s,
            pltpu.VMEM((tiles, height, width, LANES), F32),
            pltpu.VMEM((tiles, height, width, LANES), F32),
            pltpu.VMEM((2 * tiles, KS * KS + 1, 8, LANES), F32),
        ],
        10**6,
        10**5,
        "front",
    )(visible, down, down_before, down_after, depth_kernel, depth_bias, cotangent, pre)

    image_grad, small = call(
        image_kernel,
        (sd((rows, in_chans, cols), BF16), sd((64, chans), BF16)),
        [VM] * 6,
        [column, sort, pltpu.VMEM((4 * in_chans, pixels), F32), pltpu.VMEM((64, chans), F32)],
        10**6,
        10**5,
        "image",
    )(pre, weight, normed, rstd, gain, grads)
    image_grad = jnp.transpose(image_grad, (0, 2, 1))

    small, _ = lax.optimization_barrier((small, got[0]))
    tiny = [lax.ppermute(small, "rows", along_y[k]) for k in (1, 2, 3)]
    small = sum_four(small, *tiny).astype(BF16)

    half = sum_four(chunks[0], *got).astype(BF16)
    parts = [lax.dynamic_index_in_dim(half, (place_z + k) % 4, 0, False) for k in range(4)]
    got = [lax.ppermute(parts[k], "rows", along_z[k]) for k in (1, 2, 3)]
    tiny = [lax.ppermute(small, "rows", along_z[k]) for k in (1, 2, 3)]
    down_weight_grad, gain_grad, bias_grad, kernel_grad, depth_bias_grad = call(
        last_kernel,
        (
            sd((share, chans), F32),
            sd((in_chans,), F32),
            sd((chans,), F32),
            sd((KS * KS, chans), F32),
            sd((chans,), F32),
        ),
        [VM] * 8,
        [],
        10**6,
        10**6,
        "last",
    )(parts[0], *got, small, *tiny)
    return (
        features,
        image_grad,
        down_weight_grad,
        gain_grad,
        bias_grad,
        kernel_grad,
        depth_bias_grad,
    )


def solution(mesh):
    placed = (
        P(("group", "rows"), None, None),
        P(("group", "rows"), None),
        P(),
        P(),
        P(),
        P(),
        P(),
        P(("group", "rows"), None, None),
    )
    return jax.shard_map(
        body,
        mesh=mesh,
        in_specs=placed,
        out_specs=(
            P(("group", "rows"), None, None),
            P(("group", "rows"), None, None),
            P(("group", "rows"), None),
            P("group"),
            P("group"),
            P("group", None),
            P("group"),
        ),
        check_vma=False,
    )
```

```python
import functools
import math

import jax
import jax.numpy as jnp
from jax import lax
from jax.experimental import pallas as pl
from jax.experimental.pallas import tpu as pltpu
from jax.sharding import PartitionSpec as P

KS = 7
PATCH = 4
LANES = 128
F32 = jnp.float32
BF16 = jnp.bfloat16
VM = pl.BlockSpec(memory_space=pltpu.VMEM)
SM = pl.BlockSpec(memory_space=pltpu.SMEM)
ANY = pl.BlockSpec(memory_space=pl.ANY)
HBM = pl.BlockSpec(memory_space=pltpu.HBM)
FIRST = 4


def tiles_of(chans):
    return [(t, min(LANES, chans - t * LANES)) for t in range(-(-chans // LANES))]


def lanes_of(t, wd):
    return slice(t * LANES, t * LANES + wd)


def column_mask(vis, width):
    row = lax.broadcasted_iota(jnp.int32, (width, LANES), 0) // PATCH
    mask = jnp.zeros((width, LANES), F32)
    for k in range(width // PATCH):
        mask = jnp.where(row == k, vis[0, k].astype(F32), mask)
    return mask


def fetch(sources, targets, sems):
    copies = [
        pltpu.make_async_copy(source, target, sems.at[k])
        for k, (source, target) in enumerate(zip(sources, targets))
    ]
    for copy in copies:
        copy.start()
    return copies


def call(kernel, out_shape, in_specs, scratch, name, vmem=16, size=10**5):
    return pl.pallas_call(
        kernel,
        out_shape=out_shape,
        in_specs=in_specs,
        out_specs=jax.tree.map(lambda _: VM, out_shape),
        scratch_shapes=scratch,
        compiler_params=pltpu.CompilerParams(vmem_limit_bytes=vmem * 2**20),
        cost_estimate=pl.CostEstimate(flops=10**6, bytes_accessed=size, transcendentals=0),
        name=name,
    )


def edge_kernel(vis_in, cot_in, first, last, mask_out, vis, cot, sems):
    copies = fetch((vis_in, cot_in), (vis, cot), sems)
    height, width, chans = cot.shape
    copies[0].wait()
    mask = column_mask(vis, width)
    mask_out[...] = mask
    copies[1].wait()
    for t, wd in tiles_of(chans):
        lanes = lanes_of(t, wd)
        for p in range(height):
            row = (cot[p, :, lanes].astype(F32) * mask[:, :wd]).astype(BF16)
            if p < 3:
                first[p, :, lanes] = row
            if p >= height - 3:
                last[p - (height - 3), :, lanes] = row


def sorter(width, back):
    size = 4 * width
    row = lax.broadcasted_iota(jnp.int32, (size, size), 1 if back else 0)
    col = lax.broadcasted_iota(jnp.int32, (size, size), 0 if back else 1)
    half, rest = col // (2 * width), col % (2 * width)
    source = (rest // width) * (2 * width) + 2 * (rest % width) + half
    return jnp.where(row == source, 1.0, 0.0).astype(BF16)


def gain_column(gain, column):
    column[...] = jnp.transpose(jnp.broadcast_to(gain[...][None], (LANES, gain.shape[0])))


def reduce_kernel(
    image_in, gain_in, weight_in, bias_in, mask, order,
    patches, normed, rstd, down, first, last,
    column, sort, image, gain, weight, bias, sems,
):
    copies = fetch(
        (image_in, gain_in, weight_in, bias_in), (image, gain, weight, bias), sems
    )
    rows, chans, cols = image.shape
    height, width = rows // 2, cols // 2
    sort[...] = sorter(width, False)
    copies[1].wait()
    gain_column(gain, column)
    copies[0].wait()
    for a in range(2):
        for pair in range(height // 2):
            top = 4 * pair + a
            two = jnp.concatenate([image[top], image[top + 2]], axis=1)
            x = jnp.dot(two, sort[...], preferred_element_type=F32)
            center = jnp.sum(x, axis=0, keepdims=True) * (1.0 / chans)
            x = x - center
            var = jnp.sum(x * x, axis=0, keepdims=True) * (1.0 / chans)
            inv = 1.0 / jnp.sqrt(var + 1e-06)
            x = x * inv
            lanes = lanes_of(pair, LANES)
            for b in range(2):
                k = 2 * a + b
                here = slice(k * chans, (k + 1) * chans)
                part = x[:, lanes_of(b, LANES)]
                normed[here, lanes] = part.astype(BF16)
                patches[here, lanes] = (part * column[...]).astype(BF16)
                rstd[k : k + 1, lanes] = inv[:, lanes_of(b, LANES)]
    copies[2].wait()
    copies[3].wait()
    acc = jnp.dot(weight[...], patches[...], preferred_element_type=F32)
    acc = jnp.transpose(acc) + bias[...][None]
    for t, wd in tiles_of(weight.shape[0]):
        lanes = lanes_of(t, wd)
        for p in range(height):
            row = (acc[p * width : (p + 1) * width, lanes] * mask[:, :wd]).astype(BF16)
            down[p, :, lanes] = row
            if p < 3:
                first[p, :, lanes] = row
            if p >= height - 3:
                last[p - (height - 3), :, lanes] = row


def fill_band(dst, at, ref, tiles, first=0):
    count, width = ref.shape[:2]
    for t, wd in tiles:
        d = t - first
        for k in range(count):
            if wd < LANES:
                dst[d, at + k, 8 : 8 + width, wd:LANES] = jnp.zeros((width, LANES - wd), F32)
            dst[d, at + k, 8 : 8 + width, 0:wd] = ref[k, :, lanes_of(t, wd)].astype(F32)


def clear_edges(dst):
    tiles, count, span = dst.shape[:3]
    edge = jnp.zeros((tiles, count, 8, LANES), F32)
    dst[:, :, 0:8, :] = edge
    dst[:, :, span - 8 : span, :] = edge


def own_kernel(cot_in, kernel_in, mask, order, band, taps, part, cot, kernel, sems):
    copies = fetch((cot_in, kernel_in), (cot, kernel), sems)
    height, width, chans = cot.shape
    tiles = tiles_of(chans)
    clear_edges(band)
    copies[1].wait()
    for t, wd in tiles:
        taps[t, :, :, 0:wd] = jnp.broadcast_to(
            kernel[:, lanes_of(t, wd)][:, None, :], (KS * KS, 8, wd)
        )
        if wd < LANES:
            taps[t, :, :, wd:LANES] = jnp.zeros((KS * KS, 8, LANES - wd), F32)
    copies[0].wait()
    for t, wd in tiles:
        for k in range(height):
            if wd < LANES:
                band[t, k, 8 : 8 + width, wd:LANES] = jnp.zeros((width, LANES - wd), F32)
            band[t, k, 8 : 8 + width, 0:wd] = cot[k, :, lanes_of(t, wd)].astype(F32) * mask[:, :wd]
    half = width // 2

    def step(u, carry):
        t, h = u // 2, (u % 2) * half
        acc = [jnp.zeros((half // 8, 8, LANES), F32) for _ in range(height)]
        for s in range(height):
            for j in range(KS):
                value = band[t, s, pl.ds(h + 5 + j, half), :].reshape(half // 8, 8, LANES)
                for p in range(height):
                    i = s + 3 - p
                    acc[p] = acc[p] + value * taps[t, 48 - (KS * i + j)][None]
        for p in range(height):
            part[t, p, pl.ds(pl.multiple_of(h, 8), half), :] = acc[p].reshape(half, LANES)
        return carry

    lax.fori_loop(0, 2 * len(tiles), step, 0)


def back_kernel(
    base, place, before, after, band, taps, part, mask, patches, order, order_too,
    pre, c0, c1, c2, c3, halo, total, prod,
):
    chunks = (c0, c1, c2, c3)
    height, width = part.shape[1:3]
    chans = pre.shape[1]
    tiles = tiles_of(before.shape[2])[base : base + -(-chans // LANES)]
    clear_edges(halo)
    fill_band(halo, 0, before, tiles, base)
    fill_band(halo, 3, after, tiles, base)
    half = width // 2

    def step(u, carry):
        d, h = u // 2, (u % 2) * half
        t = d + base
        here = pl.ds(pl.multiple_of(h, 8), half)
        acc = [part[t, p, here, :].reshape(half // 8, 8, LANES) for p in range(height)]
        for m in range(6):
            s = m if m < 3 else m + height
            for j in range(KS):
                value = halo[d, m, pl.ds(h + 5 + j, half), :].reshape(half // 8, 8, LANES)
                for p in range(height):
                    i = s - p
                    if 0 <= i < KS:
                        acc[p] = acc[p] + value * taps[t, 48 - (KS * i + j)][None]
        keep = mask[here, :]
        lanes = pl.ds(pl.multiple_of(d * LANES, LANES), LANES)
        for p in range(height):
            own = band[t, p, pl.ds(pl.multiple_of(h + 8, 8), half), :]
            value = own + keep * acc[p].reshape(half, LANES)
            total[pl.ds(pl.multiple_of(p * width + h, 8), half), lanes] = value
        return carry

    lax.fori_loop(0, 2 * len(tiles), step, 0)
    pre[...] = total[:, :chans].astype(BF16)
    scale = 1.0 / math.sqrt(height * 16 * width)
    depth = patches.shape[0] // 4
    share = depth // 4
    for k in range(4):
        prod[...] = scale * jnp.dot(
            patches[k * depth : (k + 1) * depth, :], pre[...], preferred_element_type=F32
        )
        for d in range(4):
            to = lax.rem(place[0] + d, 4)
            at = pl.ds(pl.multiple_of(to * share, 8), share)
            chunks[d][k] = prod[at, :].astype(BF16)


def grad_kernel(down, before, after, cots, order, grads, band, kg):
    height, width, chans = down.shape
    tiles = tiles_of(chans)
    clear_edges(band)
    fill_band(band, 0, before, tiles)
    fill_band(band, 3, down, tiles)
    fill_band(band, 3 + height, after, tiles)
    half = width // 2

    def step(u, carry):
        t, h = u // 2, (u % 2) * half
        here = pl.ds(pl.multiple_of(h + 8, 8), half)
        mine = [cots[t, p, here, :].reshape(half // 8, 8, LANES) for p in range(height)]
        for j in range(KS):
            part = [jnp.zeros((half // 8, 8, LANES), F32) for _ in range(KS)]
            for s in range(height + 6):
                value = band[t, s, pl.ds(h + 5 + j, half), :].reshape(half // 8, 8, LANES)
                for p in range(height):
                    i = s - p
                    if 0 <= i < KS:
                        part[i] = part[i] + value * mine[p]
            for i in range(KS):
                kg[u, KS * i + j] = jnp.sum(part[i], axis=0)
        kg[u, KS * KS] = sum(jnp.sum(m, axis=0) for m in mine)
        return carry

    lax.fori_loop(0, 2 * len(tiles), step, 0)
    scale = 1.0 / math.sqrt(height * 16 * width)
    for t, wd in tiles:
        term = jnp.sum(kg[2 * t] + kg[2 * t + 1], axis=1) * scale
        grads[0 : KS * KS + 1, lanes_of(t, wd)] = term[:, :wd]


def front_kernel(band, taps, bias, mask, order, features, outs):
    height, width, chans = features.shape
    tiles = tiles_of(chans)
    half = width // 2

    def step(u, carry):
        t, h = u // 2, (u % 2) * half
        acc = [jnp.zeros((half // 8, 8, LANES), F32) for _ in range(height)]
        for s in range(height + 6):
            for j in range(KS):
                value = band[t, s, pl.ds(h + 5 + j, half), :].reshape(half // 8, 8, LANES)
                for p in range(height):
                    i = s - p
                    if 0 <= i < KS:
                        acc[p] = acc[p] + value * taps[t, KS * i + j][None]
        for p in range(height):
            outs[t, p, pl.ds(pl.multiple_of(h, 8), half), :] = acc[p].reshape(half, LANES)
        return carry

    lax.fori_loop(0, 2 * len(tiles), step, 0)
    for t, wd in tiles:
        lanes = lanes_of(t, wd)
        for p in range(height):
            value = (outs[t, p, :, 0:wd] + bias[lanes][None]) * mask[:, :wd]
            own = band[t, 3 + p, 8 : 8 + width, 0:wd]
            features[p, :, lanes] = (own + value).astype(BF16)


def image_kernel(
    pre_b, pre_a, weight, normed, rstd, gain, grads, image_grad, small, column, sort, flat, sums
):
    rows, chans, cols = image_grad.shape
    height, width = rows // 2, cols // 2
    scale = 1.0 / math.sqrt(height * 16 * width)
    cut = pre_b.shape[1]
    gain_column(gain, column)
    sort[...] = sorter(width, True)
    value = jnp.dot(pre_b[...], weight[:cut, :], preferred_element_type=F32)
    value = value + jnp.dot(pre_a[...], weight[cut:, :], preferred_element_type=F32)
    flat[...] = jnp.transpose(value)
    gain_sum = jnp.zeros((chans, LANES), F32)
    for a in range(2):
        for pair in range(height // 2):
            top = 4 * pair + a
            lanes = lanes_of(pair, LANES)
            two = []
            for b in range(2):
                k = 2 * a + b
                here = slice(k * chans, (k + 1) * chans)
                value = flat[here, lanes]
                norm = normed[here, lanes].astype(F32)
                gain_sum = gain_sum + norm * value
                g = value * column[...]
                mean_g = jnp.sum(g, axis=0, keepdims=True) * (1.0 / chans)
                mean_n = jnp.sum(g * norm, axis=0, keepdims=True) * (1.0 / chans)
                g = (g - mean_g - norm * mean_n) * rstd[k : k + 1, lanes]
                two.append(g.astype(BF16))
            out = jnp.dot(jnp.concatenate(two, axis=1), sort[...], preferred_element_type=F32)
            image_grad[top] = out[:, :cols].astype(BF16)
            image_grad[top + 2] = out[:, cols:].astype(BF16)
    ones = jnp.ones((8, pre_b.shape[0]), BF16)
    gain_row = jnp.sum(jnp.transpose(gain_sum), axis=0, keepdims=True)
    taps = KS * KS + 1
    sums[...] = jnp.zeros(sums.shape, F32)
    sums[0:taps, :] = grads[0:taps, :]
    for pre, lanes in ((pre_b, slice(0, cut)), (pre_a, slice(cut, weight.shape[0]))):
        bias_sum = jnp.dot(ones, pre[...], preferred_element_type=F32)[0:1]
        sums[taps : taps + 1, lanes] = bias_sum * scale
    sums[taps + 1 : taps + 2, 0:chans] = gain_row * scale
    small[...] = sums[...].astype(BF16)


def middle_kernel(place, c0, c1, c2, c3, order, *outs):
    for k in range(4):
        to = lax.rem(place[0] + k, 4)
        outs[k][...] = sum_four(c0[to], c1[to], c2[to], c3[to]).astype(BF16)


def last_kernel(
    b0, b1, b2, b3, a0, a1, a2, a3, t0, t1, t2, t3, weight, gain, bias, kernel, depth_bias
):
    cut = b0.shape[1]
    weight[:, :cut] = sum_four(b0[...], b1[...], b2[...], b3[...])
    weight[:, cut:] = sum_four(a0[...], a1[...], a2[...], a3[...])
    total = sum_four(t0[...], t1[...], t2[...], t3[...])
    taps = KS * KS
    kernel[...] = total[:taps]
    depth_bias[...] = total[taps]
    bias[...] = total[taps + 1]
    gain[...] = total[taps + 2, : gain.shape[0]]


def sd(shape, dtype):
    return jax.ShapeDtypeStruct(shape, dtype)


def sum_four(own, one, two, three):
    return (own.astype(F32) + two.astype(F32)) + (one.astype(F32) + three.astype(F32))


def send(values, pairs):
    return [lax.ppermute(value, "rows", pair) for value, pair in zip(values, pairs)]


def body(image, visible, layer_norm_gain, reducer_weight, reducer_bias, depth_kernel, depth_bias, cotangent):
    height, width, chans = cotangent.shape
    rows, cols, in_chans = image.shape
    image = jnp.transpose(image, (0, 2, 1))
    weight = jnp.transpose(reducer_weight)
    pixels = height * width
    bands = lax.axis_size("rows")
    index = lax.axis_index("rows")
    place_y = (index % 4).reshape(1).astype(jnp.int32)
    place_z = (index // 4).reshape(1).astype(jnp.int32)
    up = [(i, i + 1) for i in range(bands - 1)]
    low = [(j, i) for i, j in up]
    ring = [(z, y) for z in range(4) for y in range(4)]
    along_y = [[(4 * z + y, 4 * z + (y + k) % 4) for z, y in ring] for k in (1, 2, 3)]
    along_z = [[(4 * z + y, 4 * ((z + k) % 4) + y) for z, y in ring] for k in (1, 2, 3)]
    tiles = len(tiles_of(chans))
    cut = FIRST * LANES
    share = in_chans // 4
    halo = sd((3, width, chans), BF16)
    span = width + 16

    cot_first, cot_last, mask = call(
        edge_kernel,
        (halo, halo, sd((width, LANES), F32)),
        [HBM, HBM],
        [
            pltpu.SMEM((1, width // PATCH), jnp.int32),
            pltpu.VMEM((height, width, chans), BF16),
            pltpu.SemaphoreType.DMA((2,)),
        ],
        "edge",
        60,
        2 * 10**7,
    )(visible, cotangent)
    cot_before = lax.ppermute(cot_last, "rows", up)
    cot_after = lax.ppermute(cot_first, "rows", low)

    column = pltpu.VMEM((in_chans, LANES), F32)
    sort = pltpu.VMEM((4 * width, 4 * width), BF16)
    patches, normed, rstd, down, down_first, down_last = call(
        reduce_kernel,
        (
            sd((4 * in_chans, pixels), BF16),
            sd((4 * in_chans, pixels), BF16),
            sd((8, pixels), F32),
            sd((height, width, chans), BF16),
            halo,
            halo,
        ),
        [HBM, HBM, HBM, HBM, VM, ANY],
        [
            column,
            sort,
            pltpu.VMEM(image.shape, BF16),
            pltpu.VMEM((in_chans,), F32),
            pltpu.VMEM(weight.shape, BF16),
            pltpu.VMEM((chans,), F32),
            pltpu.SemaphoreType.DMA((4,)),
        ],
        "reduce",
        60,
        2 * 10**7,
    )(image, layer_norm_gain, weight, reducer_bias, mask, cot_first)
    down_before = lax.ppermute(down_last, "rows", up)
    down_after = lax.ppermute(down_first, "rows", low)

    band, taps, part = call(
        own_kernel,
        (
            sd((tiles, height, span, LANES), F32),
            sd((tiles, KS * KS, 8, LANES), F32),
            sd((tiles, height, width, LANES), F32),
        ),
        [HBM, HBM, VM, ANY],
        [
            pltpu.VMEM((height, width, chans), BF16),
            pltpu.VMEM((KS * KS, chans), F32),
            pltpu.SemaphoreType.DMA((2,)),
        ],
        "own",
    )(cotangent, depth_kernel, mask, down_first)

    def back(here, *order):
        size = here[1] - here[0]
        count = -(-size // LANES)
        return call(
            functools.partial(back_kernel, here[0] // LANES),
            (sd((pixels, size), BF16),) + (sd((4, share, size), BF16),) * 4,
            [SM] + [VM] * 7 + [ANY] * 2,
            [
                pltpu.VMEM((count, 6, span, LANES), F32),
                pltpu.VMEM((pixels, count * LANES), F32),
                pltpu.VMEM((in_chans, size), F32),
            ],
            "back",
        )(place_y, cot_before, cot_after, band, taps, part, mask, patches, *order)

    pre_b, *chunks_b = back((0, cut), mask, mask)
    chunks_b, down_before, down_after = lax.optimization_barrier(
        (chunks_b, down_before, down_after)
    )
    got_b = send(chunks_b[1:], along_y)
    pre_a, *chunks_a = back((cut, chans), pre_b, mask)

    grads, down_band = call(
        grad_kernel,
        (sd((56, chans), F32), sd((tiles, height + 6, span, LANES), F32)),
        [VM] * 4 + [ANY],
        [pltpu.VMEM((2 * tiles, KS * KS + 1, 8, LANES), F32)],
        "grads",
    )(down, down_before, down_after, band, pre_a)
    image_grad, small = call(
        image_kernel,
        (sd((rows, in_chans, cols), BF16), sd((56, chans), BF16)),
        [VM] * 7,
        [column, sort, pltpu.VMEM((4 * in_chans, pixels), F32), pltpu.VMEM((56, chans), F32)],
        "image",
    )(pre_b, pre_a, weight, normed, rstd, layer_norm_gain, grads)
    image_grad = jnp.transpose(image_grad, (0, 2, 1))
    features = call(
        front_kernel,
        sd((height, width, chans), BF16),
        [VM] * 4 + [ANY],
        [pltpu.VMEM((tiles, height, width, LANES), F32)],
        "front",
    )(down_band, taps, depth_bias, mask, small)

    def middle(own, got, size, order):
        return call(
            middle_kernel,
            (sd((share, size), BF16),) * 4,
            [SM] + [VM] * 4 + [ANY],
            [],
            "middle",
        )(place_z, own, *got, order)

    chunks_a[3], _ = lax.optimization_barrier((chunks_a[3], features))
    got_a = send(chunks_a[1:], along_y)
    small, *got_b = lax.optimization_barrier((small, *got_b))
    got_t = send([small] * 3, along_y)
    parts_b = middle(chunks_b[0], got_b, cut, features)
    last_b = send(parts_b[1:], along_z)
    small, *got_t = lax.optimization_barrier((small, *got_t, last_b[0]))[:4]
    small = sum_four(small, *got_t).astype(BF16)
    got_t = send([small] * 3, along_z)
    parts_a = middle(chunks_a[0], got_a, chans - cut, parts_b[0])
    last_a = send(parts_a[1:], along_z)
    down_weight_grad, gain_grad, bias_grad, kernel_grad, depth_bias_grad = call(
        last_kernel,
        (
            sd((share, chans), F32),
            sd((in_chans,), F32),
            sd((chans,), F32),
            sd((KS * KS, chans), F32),
            sd((chans,), F32),
        ),
        [VM] * 12,
        [],
        "last",
    )(parts_b[0], *last_b, parts_a[0], *last_a, small, *got_t)
    return (
        features,
        image_grad,
        down_weight_grad,
        gain_grad,
        bias_grad,
        kernel_grad,
        depth_bias_grad,
    )


def solution(mesh):
    placed = (
        P(("group", "rows"), None, None),
        P(("group", "rows"), None),
        P(),
        P(),
        P(),
        P(),
        P(),
        P(("group", "rows"), None, None),
    )
    return jax.shard_map(
        body,
        mesh=mesh,
        in_specs=placed,
        out_specs=(
            P(("group", "rows"), None, None),
            P(("group", "rows"), None, None),
            P(("group", "rows"), None),
            P("group"),
            P("group"),
            P("group", None),
            P("group"),
        ),
        check_vma=False,
    )
```

```python
import math

import jax
import jax.numpy as jnp
from jax import lax
from jax.experimental import pallas as pl
from jax.experimental.pallas import tpu as pltpu
from jax.sharding import PartitionSpec as P

KS = 7
PATCH = 4
LANES = 128
F32 = jnp.float32
BF16 = jnp.bfloat16
VM = pl.BlockSpec(memory_space=pltpu.VMEM)
SM = pl.BlockSpec(memory_space=pltpu.SMEM)
ANY = pl.BlockSpec(memory_space=pl.ANY)
HBM = pl.BlockSpec(memory_space=pltpu.HBM)


def tiles_of(chans):
    return [(t, min(LANES, chans - t * LANES)) for t in range(-(-chans // LANES))]


def lanes_of(t, wd):
    return slice(t * LANES, t * LANES + wd)


def column_mask(vis, width):
    row = lax.broadcasted_iota(jnp.int32, (width, LANES), 0) // PATCH
    mask = jnp.zeros((width, LANES), F32)
    for k in range(width // PATCH):
        mask = jnp.where(row == k, vis[0, k].astype(F32), mask)
    return mask


def fetch(sources, targets, sems):
    copies = [
        pltpu.make_async_copy(source, target, sems.at[k])
        for k, (source, target) in enumerate(zip(sources, targets))
    ]
    for copy in copies:
        copy.start()
    return copies


def call(kernel, out_shape, in_specs, scratch, name, vmem=16, size=10**5):
    return pl.pallas_call(
        kernel,
        out_shape=out_shape,
        in_specs=in_specs,
        out_specs=jax.tree.map(lambda _: VM, out_shape),
        scratch_shapes=scratch,
        compiler_params=pltpu.CompilerParams(vmem_limit_bytes=vmem * 2**20),
        cost_estimate=pl.CostEstimate(flops=10**6, bytes_accessed=size, transcendentals=0),
        name=name,
    )


def sorter(width, back):
    size = 4 * width
    row = lax.broadcasted_iota(jnp.int32, (size, size), 1 if back else 0)
    col = lax.broadcasted_iota(jnp.int32, (size, size), 0 if back else 1)
    half, rest = col // (2 * width), col % (2 * width)
    source = (rest // width) * (2 * width) + 2 * (rest % width) + half
    return jnp.where(row == source, 1.0, 0.0).astype(BF16)


def gain_column(gain, column):
    column[...] = jnp.transpose(jnp.broadcast_to(gain[...][None], (LANES, gain.shape[0])))


def reduce_kernel(
    vis_in, cot_in, image_in, gain_in, weight_in, bias_in,
    cot_first, cot_last, mask, patches, normed, rstd, down, first, last,
    column, sort, vis, cot, image, gain, weight, bias, sems,
):
    copies = fetch(
        (image_in, gain_in, weight_in, bias_in, vis_in, cot_in),
        (image, gain, weight, bias, vis, cot),
        sems,
    )
    rows, chans, cols = image.shape
    height, width = rows // 2, cols // 2
    copies[4].wait()
    mask[...] = column_mask(vis, width)
    copies[5].wait()
    for t, wd in tiles_of(cot.shape[2]):
        lanes = lanes_of(t, wd)
        for p in range(height):
            row = (cot[p, :, lanes].astype(F32) * mask[:, :wd]).astype(BF16)
            if p < 3:
                cot_first[p, :, lanes] = row
            if p >= height - 3:
                cot_last[p - (height - 3), :, lanes] = row
    sort[...] = sorter(width, False)
    copies[1].wait()
    gain_column(gain, column)
    copies[0].wait()
    for a in range(2):
        for pair in range(height // 2):
            top = 4 * pair + a
            two = jnp.concatenate([image[top], image[top + 2]], axis=1)
            x = jnp.dot(two, sort[...], preferred_element_type=F32)
            center = jnp.sum(x, axis=0, keepdims=True) * (1.0 / chans)
            x = x - center
            var = jnp.sum(x * x, axis=0, keepdims=True) * (1.0 / chans)
            inv = 1.0 / jnp.sqrt(var + 1e-06)
            x = x * inv
            lanes = lanes_of(pair, LANES)
            for b in range(2):
                k = 2 * a + b
                here = slice(k * chans, (k + 1) * chans)
                part = x[:, lanes_of(b, LANES)]
                normed[here, lanes] = part.astype(BF16)
                patches[here, lanes] = (part * column[...]).astype(BF16)
                rstd[k : k + 1, lanes] = inv[:, lanes_of(b, LANES)]
    copies[2].wait()
    copies[3].wait()
    acc = jnp.dot(weight[...], patches[...], preferred_element_type=F32)
    acc = jnp.transpose(acc) + bias[...][None]
    for t, wd in tiles_of(weight.shape[0]):
        lanes = lanes_of(t, wd)
        for p in range(height):
            row = (acc[p * width : (p + 1) * width, lanes] * mask[:, :wd]).astype(BF16)
            down[p, :, lanes] = row
            if p < 3:
                first[p, :, lanes] = row
            if p >= height - 3:
                last[p - (height - 3), :, lanes] = row


def fill_band(dst, at, ref, tiles):
    count, width = ref.shape[:2]
    for t, wd in tiles:
        for k in range(count):
            if wd < LANES:
                dst[t, at + k, 8 : 8 + width, wd:LANES] = jnp.zeros((width, LANES - wd), F32)
            dst[t, at + k, 8 : 8 + width, 0:wd] = ref[k, :, lanes_of(t, wd)].astype(F32)


def clear_edges(dst):
    tiles, count, span = dst.shape[:3]
    edge = jnp.zeros((tiles, count, 8, LANES), F32)
    dst[:, :, 0:8, :] = edge
    dst[:, :, span - 8 : span, :] = edge


def own_kernel(cot_in, kernel_in, mask, band, taps, part, cot, kernel, sems):
    copies = fetch((cot_in, kernel_in), (cot, kernel), sems)
    height, width, chans = cot.shape
    tiles = tiles_of(chans)
    clear_edges(band)
    copies[1].wait()
    for t, wd in tiles:
        taps[t, :, :, 0:wd] = jnp.broadcast_to(
            kernel[:, lanes_of(t, wd)][:, None, :], (KS * KS, 8, wd)
        )
        if wd < LANES:
            taps[t, :, :, wd:LANES] = jnp.zeros((KS * KS, 8, LANES - wd), F32)
    copies[0].wait()
    for t, wd in tiles:
        for k in range(height):
            if wd < LANES:
                band[t, k, 8 : 8 + width, wd:LANES] = jnp.zeros((width, LANES - wd), F32)
            band[t, k, 8 : 8 + width, 0:wd] = cot[k, :, lanes_of(t, wd)].astype(F32) * mask[:, :wd]
    half = width // 2

    def step(u, carry):
        t, h = u // 2, (u % 2) * half
        acc = [jnp.zeros((half // 8, 8, LANES), F32) for _ in range(height)]
        for s in range(height):
            for j in range(KS):
                value = band[t, s, pl.ds(h + 5 + j, half), :].reshape(half // 8, 8, LANES)
                for p in range(height):
                    i = s + 3 - p
                    acc[p] = acc[p] + value * taps[t, 48 - (KS * i + j)][None]
        for p in range(height):
            part[t, p, pl.ds(pl.multiple_of(h, 8), half), :] = acc[p].reshape(half, LANES)
        return carry

    lax.fori_loop(0, 2 * len(tiles), step, 0)


def back_kernel(
    place, before, after, band, taps, part, mask, patches,
    pre, c0, c1, c2, c3, halo, total, prod,
):
    chunks = (c0, c1, c2, c3)
    height, width = part.shape[1:3]
    chans = pre.shape[1]
    tiles = tiles_of(chans)
    clear_edges(halo)
    fill_band(halo, 0, before, tiles)
    fill_band(halo, 3, after, tiles)
    half = width // 2

    def step(u, carry):
        t, h = u // 2, (u % 2) * half
        here = pl.ds(pl.multiple_of(h, 8), half)
        acc = [part[t, p, here, :].reshape(half // 8, 8, LANES) for p in range(height)]
        for m in range(6):
            s = m if m < 3 else m + height
            for j in range(KS):
                value = halo[t, m, pl.ds(h + 5 + j, half), :].reshape(half // 8, 8, LANES)
                for p in range(height):
                    i = s - p
                    if 0 <= i < KS:
                        acc[p] = acc[p] + value * taps[t, 48 - (KS * i + j)][None]
        keep = mask[here, :]
        lanes = pl.ds(pl.multiple_of(t * LANES, LANES), LANES)
        for p in range(height):
            own = band[t, p, pl.ds(pl.multiple_of(h + 8, 8), half), :]
            value = own + keep * acc[p].reshape(half, LANES)
            total[pl.ds(pl.multiple_of(p * width + h, 8), half), lanes] = value
        return carry

    lax.fori_loop(0, 2 * len(tiles), step, 0)
    pre[...] = total[:, :chans].astype(BF16)
    scale = 1.0 / math.sqrt(height * 16 * width)
    depth = patches.shape[0] // 4
    share = depth // 4
    for k in range(4):
        prod[...] = scale * jnp.dot(
            patches[k * depth : (k + 1) * depth, :], pre[...], preferred_element_type=F32
        )
        for d in range(4):
            to = lax.rem(place[0] + d, 4)
            at = pl.ds(pl.multiple_of(to * share, 8), share)
            chunks[d][k] = prod[at, :].astype(BF16)


def grad_kernel(down, cots, halo, grads, band, kg):
    height, width, chans = down.shape
    tiles = tiles_of(chans)
    clear_edges(band)
    fill_band(band, 0, down, tiles)
    half = width // 2

    def step(u, carry):
        t, h = u // 2, (u % 2) * half
        here = pl.ds(pl.multiple_of(h + 8, 8), half)
        mine = [halo[t, m, here, :] for m in range(3)]
        mine += [cots[t, p, here, :] for p in range(height)]
        mine += [halo[t, m, here, :] for m in range(3, 6)]
        mine = [m.reshape(half // 8, 8, LANES) for m in mine]
        for j in range(KS):
            part = [jnp.zeros((8, LANES), F32) for _ in range(KS)]
            for r in range(height):
                value = band[t, r, pl.ds(h + 5 + j, half), :].reshape(half // 8, 8, LANES)
                for i in range(KS):
                    part[i] = part[i] + jnp.sum(value * mine[r + 6 - i], axis=0)
            for i in range(KS):
                kg[u, KS * i + j] = part[i]
        kg[u, KS * KS] = sum(jnp.sum(m, axis=0) for m in mine[3 : 3 + height])
        return carry

    lax.fori_loop(0, 2 * len(tiles), step, 0)
    scale = 1.0 / math.sqrt(height * 16 * width)
    for t, wd in tiles:
        term = jnp.sum(kg[2 * t] + kg[2 * t + 1], axis=1) * scale
        grads[0 : KS * KS + 1, lanes_of(t, wd)] = term[:, :wd]


def front_kernel(down, before, after, taps, bias, mask, features, outs, band):
    height, width, chans = features.shape
    tiles = tiles_of(chans)
    clear_edges(band)
    fill_band(band, 0, before, tiles)
    fill_band(band, 3, down, tiles)
    fill_band(band, 3 + height, after, tiles)
    half = width // 2

    def step(u, carry):
        t, h = u // 2, (u % 2) * half
        acc = [jnp.zeros((half // 8, 8, LANES), F32) for _ in range(height)]
        for s in range(height + 6):
            for j in range(KS):
                value = band[t, s, pl.ds(h + 5 + j, half), :].reshape(half // 8, 8, LANES)
                for p in range(height):
                    i = s - p
                    if 0 <= i < KS:
                        acc[p] = acc[p] + value * taps[t, KS * i + j][None]
        for p in range(height):
            outs[t, p, pl.ds(pl.multiple_of(h, 8), half), :] = acc[p].reshape(half, LANES)
        return carry

    lax.fori_loop(0, 2 * len(tiles), step, 0)
    for t, wd in tiles:
        lanes = lanes_of(t, wd)
        for p in range(height):
            value = (outs[t, p, :, 0:wd] + bias[lanes][None]) * mask[:, :wd]
            own = band[t, 3 + p, 8 : 8 + width, 0:wd]
            features[p, :, lanes] = (own + value).astype(BF16)


def image_kernel(
    pre, weight, normed, rstd, gain, grads, image_grad, small, column, sort, flat, sums
):
    rows, chans, cols = image_grad.shape
    height, width = rows // 2, cols // 2
    scale = 1.0 / math.sqrt(height * 16 * width)
    gain_column(gain, column)
    sort[...] = sorter(width, True)
    value = jnp.dot(pre[...], weight[...], preferred_element_type=F32)
    flat[...] = jnp.transpose(value)
    gain_sum = jnp.zeros((chans, LANES), F32)
    for a in range(2):
        for pair in range(height // 2):
            top = 4 * pair + a
            lanes = lanes_of(pair, LANES)
            two = []
            for b in range(2):
                k = 2 * a + b
                here = slice(k * chans, (k + 1) * chans)
                value = flat[here, lanes]
                norm = normed[here, lanes].astype(F32)
                gain_sum = gain_sum + norm * value
                g = value * column[...]
                mean_g = jnp.sum(g, axis=0, keepdims=True) * (1.0 / chans)
                mean_n = jnp.sum(g * norm, axis=0, keepdims=True) * (1.0 / chans)
                g = (g - mean_g - norm * mean_n) * rstd[k : k + 1, lanes]
                two.append(g.astype(BF16))
            out = jnp.dot(jnp.concatenate(two, axis=1), sort[...], preferred_element_type=F32)
            image_grad[top] = out[:, :cols].astype(BF16)
            image_grad[top + 2] = out[:, cols:].astype(BF16)
    ones = jnp.ones((8, pre.shape[0]), BF16)
    gain_row = jnp.sum(jnp.transpose(gain_sum), axis=0, keepdims=True)
    taps = KS * KS + 1
    sums[...] = jnp.zeros(sums.shape, F32)
    sums[0:taps, :] = grads[0:taps, :]
    bias_sum = jnp.dot(ones, pre[...], preferred_element_type=F32)[0:1]
    sums[taps : taps + 1, :] = bias_sum * scale
    sums[taps + 1 : taps + 2, 0:chans] = gain_row * scale
    small[...] = sums[...].astype(BF16)


def middle_kernel(place, c0, c1, c2, c3, *outs):
    for k in range(4):
        to = lax.rem(place[0] + k, 4)
        outs[k][...] = sum_four(c0[to], c1[to], c2[to], c3[to]).astype(BF16)


def last_kernel(
    w0, w1, w2, w3, t0, t1, t2, t3,
    weight, gain, bias, kernel, depth_bias,
):
    weight[...] = sum_four(w0[...], w1[...], w2[...], w3[...])
    total = sum_four(t0[...], t1[...], t2[...], t3[...])
    taps = KS * KS
    kernel[...] = total[:taps]
    depth_bias[...] = total[taps]
    bias[...] = total[taps + 1]
    gain[...] = total[taps + 2, : gain.shape[0]]


def sd(shape, dtype):
    return jax.ShapeDtypeStruct(shape, dtype)


def sum_four(own, one, two, three):
    return (own.astype(F32) + two.astype(F32)) + (one.astype(F32) + three.astype(F32))


def send(values, pairs):
    return [lax.ppermute(value, "rows", pair) for value, pair in zip(values, pairs)]


def body(image, visible, layer_norm_gain, reducer_weight, reducer_bias, depth_kernel, depth_bias, cotangent):
    height, width, chans = cotangent.shape
    rows, cols, in_chans = image.shape
    image = jnp.transpose(image, (0, 2, 1))
    weight = jnp.transpose(reducer_weight)
    pixels = height * width
    bands = lax.axis_size("rows")
    index = lax.axis_index("rows")
    place_y = (index % 4).reshape(1).astype(jnp.int32)
    place_z = (index // 4).reshape(1).astype(jnp.int32)
    up = [(i, i + 1) for i in range(bands - 1)]
    low = [(j, i) for i, j in up]
    ring = [(z, y) for z in range(4) for y in range(4)]
    along_y = [[(4 * z + y, 4 * z + (y + k) % 4) for z, y in ring] for k in (1, 2, 3)]
    along_z = [[(4 * z + y, 4 * ((z + k) % 4) + y) for z, y in ring] for k in (1, 2, 3)]
    tiles = len(tiles_of(chans))
    share = in_chans // 4
    halo = sd((3, width, chans), BF16)
    span = width + 16

    column = pltpu.VMEM((in_chans, LANES), F32)
    sort = pltpu.VMEM((4 * width, 4 * width), BF16)
    cot_first, cot_last, mask, patches, normed, rstd, down, down_first, down_last = call(
        reduce_kernel,
        (
            halo,
            halo,
            sd((width, LANES), F32),
            sd((4 * in_chans, pixels), BF16),
            sd((4 * in_chans, pixels), BF16),
            sd((8, pixels), F32),
            sd((height, width, chans), BF16),
            halo,
            halo,
        ),
        [HBM] * 6,
        [
            column,
            sort,
            pltpu.SMEM((1, width // PATCH), jnp.int32),
            pltpu.VMEM((height, width, chans), BF16),
            pltpu.VMEM(image.shape, BF16),
            pltpu.VMEM((in_chans,), F32),
            pltpu.VMEM(weight.shape, BF16),
            pltpu.VMEM((chans,), F32),
            pltpu.SemaphoreType.DMA((6,)),
        ],
        "reduce",
        60,
        2 * 10**7,
    )(visible, cotangent, image, layer_norm_gain, weight, reducer_bias)
    cot_before = lax.ppermute(cot_last, "rows", up)
    cot_after = lax.ppermute(cot_first, "rows", low)
    down_before = lax.ppermute(down_last, "rows", up)
    down_after = lax.ppermute(down_first, "rows", low)

    band, taps, part = call(
        own_kernel,
        (
            sd((tiles, height, span, LANES), F32),
            sd((tiles, KS * KS, 8, LANES), F32),
            sd((tiles, height, width, LANES), F32),
        ),
        [HBM, HBM, VM],
        [
            pltpu.VMEM((height, width, chans), BF16),
            pltpu.VMEM((KS * KS, chans), F32),
            pltpu.SemaphoreType.DMA((2,)),
        ],
        "own",
        16,
        10**7,
    )(cotangent, depth_kernel, mask)
    pre, *chunks, halo_rows = call(
        back_kernel,
        (sd((pixels, chans), BF16),)
        + (sd((4, share, chans), BF16),) * 4
        + (sd((tiles, 6, span, LANES), F32),),
        [SM] + [VM] * 7,
        [pltpu.VMEM((pixels, tiles * LANES), F32), pltpu.VMEM((in_chans, chans), F32)],
        "back",
    )(place_y, cot_before, cot_after, band, taps, part, mask, patches)
    chunks, down_before, down_after = lax.optimization_barrier((chunks, down_before, down_after))
    got = send(chunks[1:], along_y)

    grads = call(
        grad_kernel,
        sd((56, chans), F32),
        [VM] * 3,
        [
            pltpu.VMEM((tiles, height, span, LANES), F32),
            pltpu.VMEM((2 * tiles, KS * KS + 1, 8, LANES), F32),
        ],
        "grads",
    )(down, band, halo_rows)
    image_grad, small = call(
        image_kernel,
        (sd((rows, in_chans, cols), BF16), sd((56, chans), BF16)),
        [VM] * 6,
        [column, sort, pltpu.VMEM((4 * in_chans, pixels), F32), pltpu.VMEM((56, chans), F32)],
        "image",
    )(pre, weight, normed, rstd, layer_norm_gain, grads)
    image_grad = jnp.transpose(image_grad, (0, 2, 1))
    got_t = send([small] * 3, along_z)
    parts = call(
        middle_kernel,
        (sd((share, chans), BF16),) * 4,
        [SM] + [VM] * 4,
        [],
        "middle",
        16,
        4 * 10**7,
    )(place_z, chunks[0], *got)
    got_w = send(parts[1:], along_z)
    front_mask, _ = lax.optimization_barrier((mask, parts[0]))
    features = call(
        front_kernel,
        sd((height, width, chans), BF16),
        [VM] * 6,
        [
            pltpu.VMEM((tiles, height, width, LANES), F32),
            pltpu.VMEM((tiles, height + 6, span, LANES), F32),
        ],
        "front",
        16,
        10**7,
    )(down, down_before, down_after, taps, depth_bias, front_mask)
    small = sum_four(small, *got_t).astype(BF16)
    got_t = send([small] * 3, along_y)
    down_weight_grad, gain_grad, bias_grad, kernel_grad, depth_bias_grad = call(
        last_kernel,
        (
            sd((share, chans), F32),
            sd((in_chans,), F32),
            sd((chans,), F32),
            sd((KS * KS, chans), F32),
            sd((chans,), F32),
        ),
        [VM] * 8,
        [],
        "last",
    )(parts[0], *got_w, small, *got_t)
    return (
        features,
        image_grad,
        down_weight_grad,
        gain_grad,
        bias_grad,
        kernel_grad,
        depth_bias_grad,
    )


def solution(mesh):
    placed = (
        P(("group", "rows"), None, None),
        P(("group", "rows"), None),
        P(),
        P(),
        P(),
        P(),
        P(),
        P(("group", "rows"), None, None),
    )
    return jax.shard_map(
        body,
        mesh=mesh,
        in_specs=placed,
        out_specs=(
            P(("group", "rows"), None, None),
            P(("group", "rows"), None, None),
            P(("group", "rows"), None),
            P("group"),
            P("group"),
            P("group", None),
            P("group"),
        ),
        check_vma=False,
    )
```

```python
import math

import jax
import jax.numpy as jnp
from jax import lax
from jax.experimental import pallas as pl
from jax.experimental.pallas import tpu as pltpu
from jax.sharding import PartitionSpec as P

KS = 7
PATCH = 4
LANES = 128
F32 = jnp.float32
BF16 = jnp.bfloat16
VM = pl.BlockSpec(memory_space=pltpu.VMEM)
SM = pl.BlockSpec(memory_space=pltpu.SMEM)
HBM = pl.BlockSpec(memory_space=pltpu.HBM)


def tiles_of(chans):
    return [(t, min(LANES, chans - t * LANES)) for t in range(-(-chans // LANES))]


def lanes_of(t, wd):
    return slice(t * LANES, t * LANES + wd)


def column_mask(vis, width):
    row = lax.broadcasted_iota(jnp.int32, (width, LANES), 0) // PATCH
    mask = jnp.zeros((width, LANES), F32)
    for k in range(width // PATCH):
        mask = jnp.where(row == k, vis[0, k].astype(F32), mask)
    return mask


def fetch(sources, targets, sems):
    copies = [
        pltpu.make_async_copy(source, target, sems.at[k])
        for k, (source, target) in enumerate(zip(sources, targets))
    ]
    for copy in copies:
        copy.start()
    return copies


def call(kernel, out_shape, in_specs, scratch, name, vmem=16, size=10**5):
    return pl.pallas_call(
        kernel,
        out_shape=out_shape,
        in_specs=in_specs,
        out_specs=jax.tree.map(lambda _: VM, out_shape),
        scratch_shapes=scratch,
        compiler_params=pltpu.CompilerParams(vmem_limit_bytes=vmem * 2**20),
        cost_estimate=pl.CostEstimate(flops=10**6, bytes_accessed=size, transcendentals=0),
        name=name,
    )


def sorter(width, back):
    size = 4 * width
    row = lax.broadcasted_iota(jnp.int32, (size, size), 1 if back else 0)
    col = lax.broadcasted_iota(jnp.int32, (size, size), 0 if back else 1)
    half, rest = col // (2 * width), col % (2 * width)
    source = (rest // width) * (2 * width) + 2 * (rest % width) + half
    return jnp.where(row == source, 1.0, 0.0).astype(BF16)


def gain_column(gain, column):
    column[...] = jnp.transpose(jnp.broadcast_to(gain[...][None], (LANES, gain.shape[0])))


def reduce_kernel(
    vis_in, cot_in, image_in, gain_in, weight_in, bias_in,
    cot_first, cot_last, patches, normed, rstd, down, first, last,
    column, sort, vis, cot, image, gain, weight, bias, sems,
):
    copies = fetch(
        (image_in, gain_in, weight_in, bias_in, vis_in, cot_in),
        (image, gain, weight, bias, vis, cot),
        sems,
    )
    rows, chans, cols = image.shape
    height, width = rows // 2, cols // 2
    copies[4].wait()
    mask = column_mask(vis, width)
    copies[5].wait()
    for t, wd in tiles_of(cot.shape[2]):
        lanes = lanes_of(t, wd)
        for p in range(height):
            row = (cot[p, :, lanes].astype(F32) * mask[:, :wd]).astype(BF16)
            if p < 3:
                cot_first[p, :, lanes] = row
            if p >= height - 3:
                cot_last[p - (height - 3), :, lanes] = row
    sort[...] = sorter(width, False)
    copies[1].wait()
    gain_column(gain, column)
    copies[0].wait()
    for a in range(2):
        for pair in range(height // 2):
            top = 4 * pair + a
            two = jnp.concatenate([image[top], image[top + 2]], axis=1)
            x = jnp.dot(two, sort[...], preferred_element_type=F32)
            center = jnp.sum(x, axis=0, keepdims=True) * (1.0 / chans)
            x = x - center
            var = jnp.sum(x * x, axis=0, keepdims=True) * (1.0 / chans)
            inv = 1.0 / jnp.sqrt(var + 1e-06)
            x = x * inv
            lanes = lanes_of(pair, LANES)
            for b in range(2):
                k = 2 * a + b
                here = slice(k * chans, (k + 1) * chans)
                part = x[:, lanes_of(b, LANES)]
                normed[here, lanes] = part.astype(BF16)
                patches[here, lanes] = (part * column[...]).astype(BF16)
                rstd[k : k + 1, lanes] = inv[:, lanes_of(b, LANES)]
    copies[2].wait()
    copies[3].wait()
    acc = jnp.dot(weight[...], patches[...], preferred_element_type=F32)
    acc = jnp.transpose(acc) + bias[...][None]
    for t, wd in tiles_of(weight.shape[0]):
        lanes = lanes_of(t, wd)
        for p in range(height):
            row = (acc[p * width : (p + 1) * width, lanes] * mask[:, :wd]).astype(BF16)
            down[p, :, lanes] = row
            if p < 3:
                first[p, :, lanes] = row
            if p >= height - 3:
                last[p - (height - 3), :, lanes] = row


def fill_band(dst, at, ref, tiles):
    count, width = ref.shape[:2]
    for t, wd in tiles:
        for k in range(count):
            if wd < LANES:
                dst[t, at + k, 8 : 8 + width, wd:LANES] = jnp.zeros((width, LANES - wd), F32)
            dst[t, at + k, 8 : 8 + width, 0:wd] = ref[k, :, lanes_of(t, wd)].astype(F32)


def clear_edges(dst):
    tiles, count, span = dst.shape[:3]
    edge = jnp.zeros((tiles, count, 8, LANES), F32)
    dst[:, :, 0:8, :] = edge
    dst[:, :, span - 8 : span, :] = edge


def own_kernel(
    vis_in, cot_in, kernel_in, band, taps, part, mask_out, vis, cot, kernel, sems
):
    copies = fetch((cot_in, kernel_in, vis_in), (cot, kernel, vis), sems)
    height, width, chans = cot.shape
    copies[2].wait()
    mask = column_mask(vis, width)
    mask_out[...] = mask
    tiles = tiles_of(chans)
    clear_edges(band)
    copies[1].wait()
    for t, wd in tiles:
        taps[t, :, :, 0:wd] = jnp.broadcast_to(
            kernel[:, lanes_of(t, wd)][:, None, :], (KS * KS, 8, wd)
        )
        if wd < LANES:
            taps[t, :, :, wd:LANES] = jnp.zeros((KS * KS, 8, LANES - wd), F32)
    copies[0].wait()
    for t, wd in tiles:
        for k in range(height):
            if wd < LANES:
                band[t, k, 8 : 8 + width, wd:LANES] = jnp.zeros((width, LANES - wd), F32)
            band[t, k, 8 : 8 + width, 0:wd] = cot[k, :, lanes_of(t, wd)].astype(F32) * mask[:, :wd]
    half = width // 2

    def step(u, carry):
        t, h = u // 2, (u % 2) * half
        acc = [jnp.zeros((half // 8, 8, LANES), F32) for _ in range(height)]
        for s in range(height):
            for j in range(KS):
                value = band[t, s, pl.ds(h + 5 + j, half), :].reshape(half // 8, 8, LANES)
                for p in range(height):
                    i = s + 3 - p
                    acc[p] = acc[p] + value * taps[t, 48 - (KS * i + j)][None]
        for p in range(height):
            part[t, p, pl.ds(pl.multiple_of(h, 8), half), :] = acc[p].reshape(half, LANES)
        return carry

    lax.fori_loop(0, 2 * len(tiles), step, 0)


def back_kernel(
    place, before, after, band, taps, part, mask, patches,
    pre, c0, c1, c2, c3, halo, total, prod,
):
    chunks = (c0, c1, c2, c3)
    height, width = part.shape[1:3]
    chans = pre.shape[1]
    tiles = tiles_of(chans)
    clear_edges(halo)
    fill_band(halo, 0, before, tiles)
    fill_band(halo, 3, after, tiles)
    half = width // 2

    def step(u, carry):
        t, h = u // 2, (u % 2) * half
        here = pl.ds(pl.multiple_of(h, 8), half)
        acc = [part[t, p, here, :].reshape(half // 8, 8, LANES) for p in range(height)]
        for m in range(6):
            s = m if m < 3 else m + height
            for j in range(KS):
                value = halo[t, m, pl.ds(h + 5 + j, half), :].reshape(half // 8, 8, LANES)
                for p in range(height):
                    i = s - p
                    if 0 <= i < KS:
                        acc[p] = acc[p] + value * taps[t, 48 - (KS * i + j)][None]
        keep = mask[here, :]
        lanes = pl.ds(pl.multiple_of(t * LANES, LANES), LANES)
        for p in range(height):
            own = band[t, p, pl.ds(pl.multiple_of(h + 8, 8), half), :]
            value = own + keep * acc[p].reshape(half, LANES)
            total[pl.ds(pl.multiple_of(p * width + h, 8), half), lanes] = value
        return carry

    lax.fori_loop(0, 2 * len(tiles), step, 0)
    pre[...] = total[:, :chans].astype(BF16)
    scale = 1.0 / math.sqrt(height * 16 * width)
    depth = patches.shape[0] // 4
    share = depth // 4
    for k in range(4):
        prod[...] = scale * jnp.dot(
            patches[k * depth : (k + 1) * depth, :], pre[...], preferred_element_type=F32
        )
        for d in range(4):
            to = lax.rem(place[0] + d, 4)
            at = pl.ds(pl.multiple_of(to * share, 8), share)
            chunks[d][k] = prod[at, :].astype(BF16)


def grad_kernel(down, cots, halo, grads, band, kg):
    height, width, chans = down.shape
    tiles = tiles_of(chans)
    clear_edges(band)
    fill_band(band, 0, down, tiles)
    half = width // 2

    def step(u, carry):
        t, h = u // 2, (u % 2) * half
        here = pl.ds(pl.multiple_of(h + 8, 8), half)
        mine = [halo[t, m, here, :] for m in range(3)]
        mine += [cots[t, p, here, :] for p in range(height)]
        mine += [halo[t, m, here, :] for m in range(3, 6)]
        mine = [m.reshape(half // 8, 8, LANES) for m in mine]
        for j in range(KS):
            part = [jnp.zeros((8, LANES), F32) for _ in range(KS)]
            for r in range(height):
                value = band[t, r, pl.ds(h + 5 + j, half), :].reshape(half // 8, 8, LANES)
                for i in range(KS):
                    part[i] = part[i] + jnp.sum(value * mine[r + 6 - i], axis=0)
            for i in range(KS):
                kg[u, KS * i + j] = part[i]
        kg[u, KS * KS] = sum(jnp.sum(m, axis=0) for m in mine[3 : 3 + height])
        return carry

    lax.fori_loop(0, 2 * len(tiles), step, 0)
    scale = 1.0 / math.sqrt(height * 16 * width)
    for t, wd in tiles:
        term = jnp.sum(kg[2 * t] + kg[2 * t + 1], axis=1) * scale
        grads[0 : KS * KS + 1, lanes_of(t, wd)] = term[:, :wd]


def front_kernel(down, before, after, taps, bias, mask, features, outs, band):
    height, width, chans = features.shape
    tiles = tiles_of(chans)
    clear_edges(band)
    fill_band(band, 0, before, tiles)
    fill_band(band, 3, down, tiles)
    fill_band(band, 3 + height, after, tiles)
    half = width // 2

    def step(u, carry):
        t, h = u // 2, (u % 2) * half
        acc = [jnp.zeros((half // 8, 8, LANES), F32) for _ in range(height)]
        for s in range(height + 6):
            for j in range(KS):
                value = band[t, s, pl.ds(h + 5 + j, half), :].reshape(half // 8, 8, LANES)
                for p in range(height):
                    i = s - p
                    if 0 <= i < KS:
                        acc[p] = acc[p] + value * taps[t, KS * i + j][None]
        for p in range(height):
            outs[t, p, pl.ds(pl.multiple_of(h, 8), half), :] = acc[p].reshape(half, LANES)
        return carry

    lax.fori_loop(0, 2 * len(tiles), step, 0)
    for t, wd in tiles:
        lanes = lanes_of(t, wd)
        for p in range(height):
            value = (outs[t, p, :, 0:wd] + bias[lanes][None]) * mask[:, :wd]
            own = band[t, 3 + p, 8 : 8 + width, 0:wd]
            features[p, :, lanes] = (own + value).astype(BF16)


def image_kernel(
    pre, weight, normed, rstd, gain, grads, image_grad, small, column, sort, flat, sums
):
    rows, chans, cols = image_grad.shape
    height, width = rows // 2, cols // 2
    scale = 1.0 / math.sqrt(height * 16 * width)
    gain_column(gain, column)
    sort[...] = sorter(width, True)
    value = jnp.dot(pre[...], weight[...], preferred_element_type=F32)
    flat[...] = jnp.transpose(value)
    gain_sum = jnp.zeros((chans, LANES), F32)
    for a in range(2):
        for pair in range(height // 2):
            top = 4 * pair + a
            lanes = lanes_of(pair, LANES)
            two = []
            for b in range(2):
                k = 2 * a + b
                here = slice(k * chans, (k + 1) * chans)
                value = flat[here, lanes]
                norm = normed[here, lanes].astype(F32)
                gain_sum = gain_sum + norm * value
                g = value * column[...]
                mean_g = jnp.sum(g, axis=0, keepdims=True) * (1.0 / chans)
                mean_n = jnp.sum(g * norm, axis=0, keepdims=True) * (1.0 / chans)
                g = (g - mean_g - norm * mean_n) * rstd[k : k + 1, lanes]
                two.append(g.astype(BF16))
            out = jnp.dot(jnp.concatenate(two, axis=1), sort[...], preferred_element_type=F32)
            image_grad[top] = out[:, :cols].astype(BF16)
            image_grad[top + 2] = out[:, cols:].astype(BF16)
    ones = jnp.ones((8, pre.shape[0]), BF16)
    gain_row = jnp.sum(jnp.transpose(gain_sum), axis=0, keepdims=True)
    taps = KS * KS + 1
    sums[...] = jnp.zeros(sums.shape, F32)
    sums[0:taps, :] = grads[0:taps, :]
    bias_sum = jnp.dot(ones, pre[...], preferred_element_type=F32)[0:1]
    sums[taps : taps + 1, :] = bias_sum * scale
    sums[taps + 1 : taps + 2, 0:chans] = gain_row * scale
    small[...] = sums[...].astype(BF16)


def middle_kernel(place, c0, c1, c2, c3, *outs):
    for k in range(4):
        to = lax.rem(place[0] + k, 4)
        outs[k][...] = sum_four(c0[to], c1[to], c2[to], c3[to]).astype(BF16)


def last_kernel(
    w0, w1, w2, w3, t0, t1, t2, t3,
    weight, gain, bias, kernel, depth_bias,
):
    weight[...] = sum_four(w0[...], w1[...], w2[...], w3[...])
    total = sum_four(t0[...], t1[...], t2[...], t3[...])
    taps = KS * KS
    kernel[...] = total[:taps]
    depth_bias[...] = total[taps]
    bias[...] = total[taps + 1]
    gain[...] = total[taps + 2, : gain.shape[0]]


def sd(shape, dtype):
    return jax.ShapeDtypeStruct(shape, dtype)


def sum_four(own, one, two, three):
    return (own.astype(F32) + two.astype(F32)) + (one.astype(F32) + three.astype(F32))


def send(values, pairs):
    return [lax.ppermute(value, "rows", pair) for value, pair in zip(values, pairs)]


def body(image, visible, layer_norm_gain, reducer_weight, reducer_bias, depth_kernel, depth_bias, cotangent):
    height, width, chans = cotangent.shape
    rows, cols, in_chans = image.shape
    image = jnp.transpose(image, (0, 2, 1))
    weight = jnp.transpose(reducer_weight)
    pixels = height * width
    bands = lax.axis_size("rows")
    index = lax.axis_index("rows")
    place_y = (index % 4).reshape(1).astype(jnp.int32)
    place_z = (index // 4).reshape(1).astype(jnp.int32)
    up = [(i, i + 1) for i in range(bands - 1)]
    low = [(j, i) for i, j in up]
    ring = [(z, y) for z in range(4) for y in range(4)]
    along_y = [[(4 * z + y, 4 * z + (y + k) % 4) for z, y in ring] for k in (1, 2, 3)]
    along_z = [[(4 * z + y, 4 * ((z + k) % 4) + y) for z, y in ring] for k in (1, 2, 3)]
    tiles = len(tiles_of(chans))
    share = in_chans // 4
    halo = sd((3, width, chans), BF16)
    span = width + 16

    column = pltpu.VMEM((in_chans, LANES), F32)
    sort = pltpu.VMEM((4 * width, 4 * width), BF16)
    cot_first, cot_last, patches, normed, rstd, down, down_first, down_last = call(
        reduce_kernel,
        (
            halo,
            halo,
            sd((4 * in_chans, pixels), BF16),
            sd((4 * in_chans, pixels), BF16),
            sd((8, pixels), F32),
            sd((height, width, chans), BF16),
            halo,
            halo,
        ),
        [HBM] * 6,
        [
            column,
            sort,
            pltpu.SMEM((1, width // PATCH), jnp.int32),
            pltpu.VMEM((height, width, chans), BF16),
            pltpu.VMEM(image.shape, BF16),
            pltpu.VMEM((in_chans,), F32),
            pltpu.VMEM(weight.shape, BF16),
            pltpu.VMEM((chans,), F32),
            pltpu.SemaphoreType.DMA((6,)),
        ],
        "reduce",
        60,
        2 * 10**7,
    )(visible, cotangent, image, layer_norm_gain, weight, reducer_bias)
    cot_before = lax.ppermute(cot_last, "rows", up)
    cot_after = lax.ppermute(cot_first, "rows", low)
    down_before = lax.ppermute(down_last, "rows", up)
    down_after = lax.ppermute(down_first, "rows", low)

    vis_own, _ = lax.optimization_barrier((visible, rstd))
    band, taps, part, mask = call(
        own_kernel,
        (
            sd((tiles, height, span, LANES), F32),
            sd((tiles, KS * KS, 8, LANES), F32),
            sd((tiles, height, width, LANES), F32),
            sd((width, LANES), F32),
        ),
        [HBM] * 3,
        [
            pltpu.SMEM((1, width // PATCH), jnp.int32),
            pltpu.VMEM((height, width, chans), BF16),
            pltpu.VMEM((KS * KS, chans), F32),
            pltpu.SemaphoreType.DMA((3,)),
        ],
        "own",
        16,
        5 * 10**7,
    )(vis_own, cotangent, depth_kernel)

    pre, *chunks, halo_rows = call(
        back_kernel,
        (sd((pixels, chans), BF16),)
        + (sd((4, share, chans), BF16),) * 4
        + (sd((tiles, 6, span, LANES), F32),),
        [SM] + [VM] * 7,
        [pltpu.VMEM((pixels, tiles * LANES), F32), pltpu.VMEM((in_chans, chans), F32)],
        "back",
        16,
        10**9,
    )(place_y, cot_before, cot_after, band, taps, part, mask, patches)
    got = send(chunks[1:], along_y)
    down, down_before, down_after = lax.optimization_barrier((down, down_before, down_after))

    grads = call(
        grad_kernel,
        sd((56, chans), F32),
        [VM] * 3,
        [
            pltpu.VMEM((tiles, height, span, LANES), F32),
            pltpu.VMEM((2 * tiles, KS * KS + 1, 8, LANES), F32),
        ],
        "grads",
    )(down, band, halo_rows)
    image_grad, small = call(
        image_kernel,
        (sd((rows, in_chans, cols), BF16), sd((56, chans), BF16)),
        [VM] * 6,
        [column, sort, pltpu.VMEM((4 * in_chans, pixels), F32), pltpu.VMEM((56, chans), F32)],
        "image",
    )(pre, weight, normed, rstd, layer_norm_gain, grads)
    image_grad = jnp.transpose(image_grad, (0, 2, 1))
    got_t = send([small] * 3, along_z)
    parts = call(
        middle_kernel,
        (sd((share, chans), BF16),) * 4,
        [SM] + [VM] * 4,
        [],
        "middle",
        16,
        4 * 10**7,
    )(place_z, chunks[0], *got)
    got_w = send(parts[1:], along_z)
    front_mask, _ = lax.optimization_barrier((mask, parts[0]))
    features = call(
        front_kernel,
        sd((height, width, chans), BF16),
        [VM] * 6,
        [
            pltpu.VMEM((tiles, height, width, LANES), F32),
            pltpu.VMEM((tiles, height + 6, span, LANES), F32),
        ],
        "front",
        16,
        10**7,
    )(down, down_before, down_after, taps, depth_bias, front_mask)
    small = sum_four(small, *got_t).astype(BF16)
    got_t = send([small] * 3, along_y)
    down_weight_grad, gain_grad, bias_grad, kernel_grad, depth_bias_grad = call(
        last_kernel,
        (
            sd((share, chans), F32),
            sd((in_chans,), F32),
            sd((chans,), F32),
            sd((KS * KS, chans), F32),
            sd((chans,), F32),
        ),
        [VM] * 8,
        [],
        "last",
    )(parts[0], *got_w, small, *got_t)
    return (
        features,
        image_grad,
        down_weight_grad,
        gain_grad,
        bias_grad,
        kernel_grad,
        depth_bias_grad,
    )


def solution(mesh):
    placed = (
        P(("group", "rows"), None, None),
        P(("group", "rows"), None),
        P(),
        P(),
        P(),
        P(),
        P(),
        P(("group", "rows"), None, None),
    )
    return jax.shard_map(
        body,
        mesh=mesh,
        in_specs=placed,
        out_specs=(
            P(("group", "rows"), None, None),
            P(("group", "rows"), None, None),
            P(("group", "rows"), None),
            P("group"),
            P("group"),
            P("group", None),
            P("group"),
        ),
        check_vma=False,
    )
```

```python
import math

import jax
import jax.numpy as jnp
from jax import lax
from jax.experimental import pallas as pl
from jax.experimental.pallas import tpu as pltpu
from jax.sharding import PartitionSpec as P

KS = 7
PATCH = 4
LANES = 128
F32 = jnp.float32
BF16 = jnp.bfloat16
VM = pl.BlockSpec(memory_space=pltpu.VMEM)
SM = pl.BlockSpec(memory_space=pltpu.SMEM)
HBM = pl.BlockSpec(memory_space=pltpu.HBM)


def tiles_of(chans):
    return [(t, min(LANES, chans - t * LANES)) for t in range(-(-chans // LANES))]


def lanes_of(t, wd):
    return slice(t * LANES, t * LANES + wd)


def column_mask(vis, width):
    row = lax.broadcasted_iota(jnp.int32, (width, LANES), 0) // PATCH
    mask = jnp.zeros((width, LANES), F32)
    for k in range(width // PATCH):
        mask = jnp.where(row == k, vis[0, k].astype(F32), mask)
    return mask


def fetch(sources, targets, sems):
    copies = [
        pltpu.make_async_copy(source, target, sems.at[k])
        for k, (source, target) in enumerate(zip(sources, targets))
    ]
    for copy in copies:
        copy.start()
    return copies


def call(kernel, out_shape, in_specs, scratch, name, vmem=16, size=10**5):
    return pl.pallas_call(
        kernel,
        out_shape=out_shape,
        in_specs=in_specs,
        out_specs=jax.tree.map(lambda _: VM, out_shape),
        scratch_shapes=scratch,
        compiler_params=pltpu.CompilerParams(vmem_limit_bytes=vmem * 2**20),
        cost_estimate=pl.CostEstimate(flops=10**6, bytes_accessed=size, transcendentals=0),
        name=name,
    )


def sorter(width, back):
    size = 4 * width
    row = lax.broadcasted_iota(jnp.int32, (size, size), 1 if back else 0)
    col = lax.broadcasted_iota(jnp.int32, (size, size), 0 if back else 1)
    half, rest = col // (2 * width), col % (2 * width)
    source = (rest // width) * (2 * width) + 2 * (rest % width) + half
    return jnp.where(row == source, 1.0, 0.0).astype(BF16)


def gain_column(gain, column):
    column[...] = jnp.transpose(jnp.broadcast_to(gain[...][None], (LANES, gain.shape[0])))


def reduce_kernel(
    vis_in, cot_in, image_in, gain_in, weight_in, bias_in,
    cot_first, cot_last, patches, normed, rstd, down, first, last,
    column, sort, vis, cot, image, gain, weight, bias, sems,
):
    copies = fetch(
        (image_in, gain_in, weight_in, bias_in, vis_in, cot_in),
        (image, gain, weight, bias, vis, cot),
        sems,
    )
    rows, chans, cols = image.shape
    height, width = rows // 2, cols // 2
    copies[4].wait()
    mask = column_mask(vis, width)
    copies[5].wait()
    for t, wd in tiles_of(cot.shape[2]):
        lanes = lanes_of(t, wd)
        for p in range(height):
            row = (cot[p, :, lanes].astype(F32) * mask[:, :wd]).astype(BF16)
            if p < 3:
                cot_first[p, :, lanes] = row
            if p >= height - 3:
                cot_last[p - (height - 3), :, lanes] = row
    sort[...] = sorter(width, False)
    copies[1].wait()
    gain_column(gain, column)
    copies[0].wait()
    for a in range(2):
        for pair in range(height // 2):
            top = 4 * pair + a
            two = jnp.concatenate([image[top], image[top + 2]], axis=1)
            x = jnp.dot(two, sort[...], preferred_element_type=F32)
            center = jnp.sum(x, axis=0, keepdims=True) * (1.0 / chans)
            x = x - center
            var = jnp.sum(x * x, axis=0, keepdims=True) * (1.0 / chans)
            inv = 1.0 / jnp.sqrt(var + 1e-06)
            x = x * inv
            lanes = lanes_of(pair, LANES)
            for b in range(2):
                k = 2 * a + b
                here = slice(k * chans, (k + 1) * chans)
                part = x[:, lanes_of(b, LANES)]
                normed[here, lanes] = part.astype(BF16)
                patches[here, lanes] = (part * column[...]).astype(BF16)
                rstd[k : k + 1, lanes] = inv[:, lanes_of(b, LANES)]
    copies[2].wait()
    copies[3].wait()
    acc = jnp.dot(weight[...], patches[...], preferred_element_type=F32)
    acc = jnp.transpose(acc) + bias[...][None]
    for t, wd in tiles_of(weight.shape[0]):
        lanes = lanes_of(t, wd)
        for p in range(height):
            row = (acc[p * width : (p + 1) * width, lanes] * mask[:, :wd]).astype(BF16)
            down[p, :, lanes] = row
            if p < 3:
                first[p, :, lanes] = row
            if p >= height - 3:
                last[p - (height - 3), :, lanes] = row


def fill_band(dst, at, ref, tiles):
    count, width = ref.shape[:2]
    for t, wd in tiles:
        for k in range(count):
            if wd < LANES:
                dst[t, at + k, 8 : 8 + width, wd:LANES] = jnp.zeros((width, LANES - wd), F32)
            dst[t, at + k, 8 : 8 + width, 0:wd] = ref[k, :, lanes_of(t, wd)].astype(F32)


def clear_edges(dst):
    tiles, count, span = dst.shape[:3]
    edge = jnp.zeros((tiles, count, 8, LANES), F32)
    dst[:, :, 0:8, :] = edge
    dst[:, :, span - 8 : span, :] = edge


def own_kernel(
    vis_in, cot_in, kernel_in, band, taps, part, mask_out, vis, cot, kernel, sems
):
    copies = fetch((cot_in, kernel_in, vis_in), (cot, kernel, vis), sems)
    height, width, chans = cot.shape
    copies[2].wait()
    mask = column_mask(vis, width)
    mask_out[...] = mask
    tiles = tiles_of(chans)
    clear_edges(band)
    copies[1].wait()
    for t, wd in tiles:
        taps[t, :, :, 0:wd] = jnp.broadcast_to(
            kernel[:, lanes_of(t, wd)][:, None, :], (KS * KS, 8, wd)
        )
        if wd < LANES:
            taps[t, :, :, wd:LANES] = jnp.zeros((KS * KS, 8, LANES - wd), F32)
    copies[0].wait()
    for t, wd in tiles:
        for k in range(height):
            if wd < LANES:
                band[t, k, 8 : 8 + width, wd:LANES] = jnp.zeros((width, LANES - wd), F32)
            band[t, k, 8 : 8 + width, 0:wd] = cot[k, :, lanes_of(t, wd)].astype(F32) * mask[:, :wd]
    half = width // 2

    def step(u, carry):
        t, h = u // 2, (u % 2) * half
        acc = [jnp.zeros((half // 8, 8, LANES), F32) for _ in range(height)]
        for s in range(height):
            for j in range(KS):
                value = band[t, s, pl.ds(h + 5 + j, half), :].reshape(half // 8, 8, LANES)
                for p in range(height):
                    i = s + 3 - p
                    acc[p] = acc[p] + value * taps[t, 48 - (KS * i + j)][None]
        for p in range(height):
            part[t, p, pl.ds(pl.multiple_of(h, 8), half), :] = acc[p].reshape(half, LANES)
        return carry

    lax.fori_loop(0, 2 * len(tiles), step, 0)


def back_kernel(before, after, band, taps, part, mask, pre, halo, total):
    height, width = part.shape[1:3]
    chans = pre.shape[1]
    tiles = tiles_of(chans)
    clear_edges(halo)
    fill_band(halo, 0, before, tiles)
    fill_band(halo, 3, after, tiles)
    half = width // 2

    def step(u, carry):
        t, h = u // 2, (u % 2) * half
        here = pl.ds(pl.multiple_of(h, 8), half)
        acc = [part[t, p, here, :].reshape(half // 8, 8, LANES) for p in range(height)]
        for m in range(6):
            s = m if m < 3 else m + height
            for j in range(KS):
                value = halo[t, m, pl.ds(h + 5 + j, half), :].reshape(half // 8, 8, LANES)
                for p in range(height):
                    i = s - p
                    if 0 <= i < KS:
                        acc[p] = acc[p] + value * taps[t, 48 - (KS * i + j)][None]
        keep = mask[here, :]
        lanes = pl.ds(pl.multiple_of(t * LANES, LANES), LANES)
        for p in range(height):
            own = band[t, p, pl.ds(pl.multiple_of(h + 8, 8), half), :]
            value = own + keep * acc[p].reshape(half, LANES)
            total[pl.ds(pl.multiple_of(p * width + h, 8), half), lanes] = value
        return carry

    lax.fori_loop(0, 2 * len(tiles), step, 0)
    pre[...] = total[:, :chans].astype(BF16)

def product_kernel(place, patches, pre, c0, c1, c2, c3, prod):
    chunks = (c0, c1, c2, c3)
    scale = 1.0 / math.sqrt(pre.shape[0] * 16)
    depth = patches.shape[0] // 4
    share = depth // 4
    for k in range(4):
        prod[...] = scale * jnp.dot(
            patches[k * depth : (k + 1) * depth, :], pre[...], preferred_element_type=F32
        )
        for d in range(4):
            to = lax.rem(place[0] + d, 4)
            at = pl.ds(pl.multiple_of(to * share, 8), share)
            chunks[d][k] = prod[at, :].astype(BF16)


def grad_kernel(down, cots, halo, grads, band, kg):
    height, width, chans = down.shape
    tiles = tiles_of(chans)
    clear_edges(band)
    fill_band(band, 0, down, tiles)
    half = width // 2

    def step(u, carry):
        t, h = u // 2, (u % 2) * half
        here = pl.ds(pl.multiple_of(h + 8, 8), half)
        mine = [halo[t, m, here, :] for m in range(3)]
        mine += [cots[t, p, here, :] for p in range(height)]
        mine += [halo[t, m, here, :] for m in range(3, 6)]
        mine = [m.reshape(half // 8, 8, LANES) for m in mine]
        for j in range(KS):
            part = [jnp.zeros((8, LANES), F32) for _ in range(KS)]
            for r in range(height):
                value = band[t, r, pl.ds(h + 5 + j, half), :].reshape(half // 8, 8, LANES)
                for i in range(KS):
                    part[i] = part[i] + jnp.sum(value * mine[r + 6 - i], axis=0)
            for i in range(KS):
                kg[u, KS * i + j] = part[i]
        kg[u, KS * KS] = sum(jnp.sum(m, axis=0) for m in mine[3 : 3 + height])
        return carry

    lax.fori_loop(0, 2 * len(tiles), step, 0)
    scale = 1.0 / math.sqrt(height * 16 * width)
    for t, wd in tiles:
        term = jnp.sum(kg[2 * t] + kg[2 * t + 1], axis=1) * scale
        grads[0 : KS * KS + 1, lanes_of(t, wd)] = term[:, :wd]


def front_kernel(down, before, after, taps, bias, mask, features, outs, band):
    height, width, chans = features.shape
    tiles = tiles_of(chans)
    clear_edges(band)
    fill_band(band, 0, before, tiles)
    fill_band(band, 3, down, tiles)
    fill_band(band, 3 + height, after, tiles)
    half = width // 2

    def step(u, carry):
        t, h = u // 2, (u % 2) * half
        acc = [jnp.zeros((half // 8, 8, LANES), F32) for _ in range(height)]
        for s in range(height + 6):
            for j in range(KS):
                value = band[t, s, pl.ds(h + 5 + j, half), :].reshape(half // 8, 8, LANES)
                for p in range(height):
                    i = s - p
                    if 0 <= i < KS:
                        acc[p] = acc[p] + value * taps[t, KS * i + j][None]
        for p in range(height):
            outs[t, p, pl.ds(pl.multiple_of(h, 8), half), :] = acc[p].reshape(half, LANES)
        return carry

    lax.fori_loop(0, 2 * len(tiles), step, 0)
    for t, wd in tiles:
        lanes = lanes_of(t, wd)
        for p in range(height):
            value = (outs[t, p, :, 0:wd] + bias[lanes][None]) * mask[:, :wd]
            own = band[t, 3 + p, 8 : 8 + width, 0:wd]
            features[p, :, lanes] = (own + value).astype(BF16)


def image_kernel(
    pre, weight, normed, rstd, gain, grads, image_grad, small, column, sort, flat, sums
):
    rows, chans, cols = image_grad.shape
    height, width = rows // 2, cols // 2
    scale = 1.0 / math.sqrt(height * 16 * width)
    gain_column(gain, column)
    sort[...] = sorter(width, True)
    value = jnp.dot(pre[...], weight[...], preferred_element_type=F32)
    flat[...] = jnp.transpose(value)
    gain_sum = jnp.zeros((chans, LANES), F32)
    for a in range(2):
        for pair in range(height // 2):
            top = 4 * pair + a
            lanes = lanes_of(pair, LANES)
            two = []
            for b in range(2):
                k = 2 * a + b
                here = slice(k * chans, (k + 1) * chans)
                value = flat[here, lanes]
                norm = normed[here, lanes].astype(F32)
                gain_sum = gain_sum + norm * value
                g = value * column[...]
                mean_g = jnp.sum(g, axis=0, keepdims=True) * (1.0 / chans)
                mean_n = jnp.sum(g * norm, axis=0, keepdims=True) * (1.0 / chans)
                g = (g - mean_g - norm * mean_n) * rstd[k : k + 1, lanes]
                two.append(g.astype(BF16))
            out = jnp.dot(jnp.concatenate(two, axis=1), sort[...], preferred_element_type=F32)
            image_grad[top] = out[:, :cols].astype(BF16)
            image_grad[top + 2] = out[:, cols:].astype(BF16)
    ones = jnp.ones((8, pre.shape[0]), BF16)
    gain_row = jnp.sum(jnp.transpose(gain_sum), axis=0, keepdims=True)
    taps = KS * KS + 1
    sums[...] = jnp.zeros(sums.shape, F32)
    sums[0:taps, :] = grads[0:taps, :]
    bias_sum = jnp.dot(ones, pre[...], preferred_element_type=F32)[0:1]
    sums[taps : taps + 1, :] = bias_sum * scale
    sums[taps + 1 : taps + 2, 0:chans] = gain_row * scale
    small[...] = sums[...].astype(BF16)


def middle_kernel(place, c0, c1, c2, c3, *outs):
    for k in (1, 2, 3):
        to = jnp.bitwise_xor(place[0], k)
        outs[k - 1][...] = sum_four(c0[to], c1[to], c2[to], c3[to]).astype(BF16)


def last_kernel(
    place, c0, c1, c2, c3, w1, w2, w3, t0, t1, t2, t3,
    weight, gain, bias, kernel, depth_bias,
):
    z = place[0]
    own = sum_four(c0[z], c1[z], c2[z], c3[z])
    weight[...] = sum_four(own, w1[...], w2[...], w3[...])
    total = sum_four(t0[...], t1[...], t2[...], t3[...])
    taps = KS * KS
    kernel[...] = total[:taps]
    depth_bias[...] = total[taps]
    bias[...] = total[taps + 1]
    gain[...] = total[taps + 2, : gain.shape[0]]


def sd(shape, dtype):
    return jax.ShapeDtypeStruct(shape, dtype)


def sum_four(own, one, two, three):
    return (own.astype(F32) + two.astype(F32)) + (one.astype(F32) + three.astype(F32))


def send(values, pairs):
    return [lax.ppermute(value, "rows", pair) for value, pair in zip(values, pairs)]


def body(image, visible, layer_norm_gain, reducer_weight, reducer_bias, depth_kernel, depth_bias, cotangent):
    height, width, chans = cotangent.shape
    rows, cols, in_chans = image.shape
    image = jnp.transpose(image, (0, 2, 1))
    weight = jnp.transpose(reducer_weight)
    pixels = height * width
    bands = lax.axis_size("rows")
    index = lax.axis_index("rows")
    place_y = (index % 4).reshape(1).astype(jnp.int32)
    place_z = (index // 4).reshape(1).astype(jnp.int32)
    up = [(i, i + 1) for i in range(bands - 1)]
    low = [(j, i) for i, j in up]
    ring = [(z, y) for z in range(4) for y in range(4)]
    along_y = [[(4 * z + y, 4 * z + (y + k) % 4) for z, y in ring] for k in (1, 2, 3)]
    along_z = [[(4 * z + y, 4 * (z ^ k) + y) for z, y in ring] for k in (1, 2, 3)]
    tiles = len(tiles_of(chans))
    share = in_chans // 4
    halo = sd((3, width, chans), BF16)
    span = width + 16

    column = pltpu.VMEM((in_chans, LANES), F32)
    sort = pltpu.VMEM((4 * width, 4 * width), BF16)
    cot_first, cot_last, patches, normed, rstd, down, down_first, down_last = call(
        reduce_kernel,
        (
            halo,
            halo,
            sd((4 * in_chans, pixels), BF16),
            sd((4 * in_chans, pixels), BF16),
            sd((8, pixels), F32),
            sd((height, width, chans), BF16),
            halo,
            halo,
        ),
        [HBM] * 6,
        [
            column,
            sort,
            pltpu.SMEM((1, width // PATCH), jnp.int32),
            pltpu.VMEM((height, width, chans), BF16),
            pltpu.VMEM(image.shape, BF16),
            pltpu.VMEM((in_chans,), F32),
            pltpu.VMEM(weight.shape, BF16),
            pltpu.VMEM((chans,), F32),
            pltpu.SemaphoreType.DMA((6,)),
        ],
        "reduce",
        60,
        2 * 10**7,
    )(visible, cotangent, image, layer_norm_gain, weight, reducer_bias)
    cot_before = lax.ppermute(cot_last, "rows", up)
    cot_after = lax.ppermute(cot_first, "rows", low)
    down_before = lax.ppermute(down_last, "rows", up)
    down_after = lax.ppermute(down_first, "rows", low)

    vis_own, _ = lax.optimization_barrier((visible, rstd))
    band, taps, part, mask = call(
        own_kernel,
        (
            sd((tiles, height, span, LANES), F32),
            sd((tiles, KS * KS, 8, LANES), F32),
            sd((tiles, height, width, LANES), F32),
            sd((width, LANES), F32),
        ),
        [HBM] * 3,
        [
            pltpu.SMEM((1, width // PATCH), jnp.int32),
            pltpu.VMEM((height, width, chans), BF16),
            pltpu.VMEM((KS * KS, chans), F32),
            pltpu.SemaphoreType.DMA((3,)),
        ],
        "own",
        16,
        5 * 10**7,
    )(vis_own, cotangent, depth_kernel)

    pre, halo_rows = call(
        back_kernel,
        (sd((pixels, chans), BF16), sd((tiles, 6, span, LANES), F32)),
        [VM] * 6,
        [pltpu.VMEM((pixels, tiles * LANES), F32)],
        "back",
        16,
        10**9,
    )(cot_before, cot_after, band, taps, part, mask)
    chunks = call(
        product_kernel,
        [sd((4, share, chans), BF16)] * 4,
        [SM] + [VM] * 2,
        [pltpu.VMEM((in_chans, chans), F32)],
        "product",
    )(place_y, patches, pre)
    got = send(chunks[1:], along_y)
    down, down_before, down_after = lax.optimization_barrier((down, down_before, down_after))

    grads = call(
        grad_kernel,
        sd((56, chans), F32),
        [VM] * 3,
        [
            pltpu.VMEM((tiles, height, span, LANES), F32),
            pltpu.VMEM((2 * tiles, KS * KS + 1, 8, LANES), F32),
        ],
        "grads",
    )(down, band, halo_rows)
    image_grad, small = call(
        image_kernel,
        (sd((rows, in_chans, cols), BF16), sd((56, chans), BF16)),
        [VM] * 6,
        [column, sort, pltpu.VMEM((4 * in_chans, pixels), F32), pltpu.VMEM((56, chans), F32)],
        "image",
    )(pre, weight, normed, rstd, layer_norm_gain, grads)
    image_grad = jnp.transpose(image_grad, (0, 2, 1))
    got_t = send([small] * 3, along_z)
    parts = call(
        middle_kernel,
        (sd((share, chans), BF16),) * 3,
        [SM] + [VM] * 4,
        [],
        "middle",
        16,
        4 * 10**7,
    )(place_z, chunks[0], *got)
    got_w = send(parts, along_z)
    front_mask, _ = lax.optimization_barrier((mask, parts[0]))
    features = call(
        front_kernel,
        sd((height, width, chans), BF16),
        [VM] * 6,
        [
            pltpu.VMEM((tiles, height, width, LANES), F32),
            pltpu.VMEM((tiles, height + 6, span, LANES), F32),
        ],
        "front",
        16,
        10**7,
    )(down, down_before, down_after, taps, depth_bias, front_mask)
    small = sum_four(small, *got_t).astype(BF16)
    got_t = send([small] * 3, along_y)
    down_weight_grad, gain_grad, bias_grad, kernel_grad, depth_bias_grad = call(
        last_kernel,
        (
            sd((share, chans), F32),
            sd((in_chans,), F32),
            sd((chans,), F32),
            sd((KS * KS, chans), F32),
            sd((chans,), F32),
        ),
        [SM] + [VM] * 11,
        [],
        "last",
    )(place_z, chunks[0], *got, *got_w, small, *got_t)
    return (
        features,
        image_grad,
        down_weight_grad,
        gain_grad,
        bias_grad,
        kernel_grad,
        depth_bias_grad,
    )


def solution(mesh):
    placed = (
        P(("group", "rows"), None, None),
        P(("group", "rows"), None),
        P(),
        P(),
        P(),
        P(),
        P(),
        P(("group", "rows"), None, None),
    )
    return jax.shard_map(
        body,
        mesh=mesh,
        in_specs=placed,
        out_specs=(
            P(("group", "rows"), None, None),
            P(("group", "rows"), None, None),
            P(("group", "rows"), None),
            P("group"),
            P("group"),
            P("group", None),
            P("group"),
        ),
        check_vma=False,
    )
```

```python
import math

import jax
import jax.numpy as jnp
from jax import lax
from jax.experimental import pallas as pl
from jax.experimental.pallas import tpu as pltpu
from jax.sharding import PartitionSpec as P

KS = 7
PATCH = 4
LANES = 128
F32 = jnp.float32
BF16 = jnp.bfloat16
VM = pl.BlockSpec(memory_space=pltpu.VMEM)
SM = pl.BlockSpec(memory_space=pltpu.SMEM)
HBM = pl.BlockSpec(memory_space=pltpu.HBM)


def tiles_of(chans):
    return [(t, min(LANES, chans - t * LANES)) for t in range(-(-chans // LANES))]


def lanes_of(t, wd):
    return slice(t * LANES, t * LANES + wd)


def column_mask(vis, width):
    row = lax.broadcasted_iota(jnp.int32, (width, LANES), 0) // PATCH
    mask = jnp.zeros((width, LANES), F32)
    for k in range(width // PATCH):
        mask = jnp.where(row == k, vis[0, k].astype(F32), mask)
    return mask


def fetch(sources, targets, sems):
    copies = [
        pltpu.make_async_copy(source, target, sems.at[k])
        for k, (source, target) in enumerate(zip(sources, targets))
    ]
    for copy in copies:
        copy.start()
    return copies


def call(kernel, out_shape, in_specs, scratch, name, vmem=16, size=10**5):
    return pl.pallas_call(
        kernel,
        out_shape=out_shape,
        in_specs=in_specs,
        out_specs=jax.tree.map(lambda _: VM, out_shape),
        scratch_shapes=scratch,
        compiler_params=pltpu.CompilerParams(vmem_limit_bytes=vmem * 2**20),
        cost_estimate=pl.CostEstimate(flops=10**6, bytes_accessed=size, transcendentals=0),
        name=name,
    )


def sorter(width, back):
    size = 4 * width
    row = lax.broadcasted_iota(jnp.int32, (size, size), 1 if back else 0)
    col = lax.broadcasted_iota(jnp.int32, (size, size), 0 if back else 1)
    half, rest = col // (2 * width), col % (2 * width)
    source = (rest // width) * (2 * width) + 2 * (rest % width) + half
    return jnp.where(row == source, 1.0, 0.0).astype(BF16)


def gain_column(gain, column):
    column[...] = jnp.transpose(jnp.broadcast_to(gain[...][None], (LANES, gain.shape[0])))


def reduce_kernel(
    vis_in, cot_in, image_in, gain_in, weight_in, bias_in,
    cot_first, cot_last, patches, normed, rstd, down, first, last,
    column, sort, vis, cot, image, gain, weight, bias, sems,
):
    copies = fetch(
        (image_in, gain_in, weight_in, bias_in, vis_in, cot_in),
        (image, gain, weight, bias, vis, cot),
        sems,
    )
    rows, chans, cols = image.shape
    height, width = rows // 2, cols // 2
    copies[4].wait()
    mask = column_mask(vis, width)
    copies[5].wait()
    for t, wd in tiles_of(cot.shape[2]):
        lanes = lanes_of(t, wd)
        for p in range(height):
            row = (cot[p, :, lanes].astype(F32) * mask[:, :wd]).astype(BF16)
            if p < 3:
                cot_first[p, :, lanes] = row
            if p >= height - 3:
                cot_last[p - (height - 3), :, lanes] = row
    sort[...] = sorter(width, False)
    copies[1].wait()
    gain_column(gain, column)
    copies[0].wait()
    for a in range(2):
        for pair in range(height // 2):
            top = 4 * pair + a
            two = jnp.concatenate([image[top], image[top + 2]], axis=1)
            x = jnp.dot(two, sort[...], preferred_element_type=F32)
            center = jnp.sum(x, axis=0, keepdims=True) * (1.0 / chans)
            x = x - center
            var = jnp.sum(x * x, axis=0, keepdims=True) * (1.0 / chans)
            inv = 1.0 / jnp.sqrt(var + 1e-06)
            x = x * inv
            lanes = lanes_of(pair, LANES)
            for b in range(2):
                k = 2 * a + b
                here = slice(k * chans, (k + 1) * chans)
                part = x[:, lanes_of(b, LANES)]
                normed[here, lanes] = part.astype(BF16)
                patches[here, lanes] = (part * column[...]).astype(BF16)
                rstd[k : k + 1, lanes] = inv[:, lanes_of(b, LANES)]
    copies[2].wait()
    copies[3].wait()
    acc = jnp.dot(weight[...], patches[...], preferred_element_type=F32)
    acc = jnp.transpose(acc) + bias[...][None]
    for t, wd in tiles_of(weight.shape[0]):
        lanes = lanes_of(t, wd)
        for p in range(height):
            row = (acc[p * width : (p + 1) * width, lanes] * mask[:, :wd]).astype(BF16)
            down[p, :, lanes] = row
            if p < 3:
                first[p, :, lanes] = row
            if p >= height - 3:
                last[p - (height - 3), :, lanes] = row


def fill_band(dst, at, ref, tiles):
    count, width = ref.shape[:2]
    for t, wd in tiles:
        for k in range(count):
            if wd < LANES:
                dst[t, at + k, 8 : 8 + width, wd:LANES] = jnp.zeros((width, LANES - wd), F32)
            dst[t, at + k, 8 : 8 + width, 0:wd] = ref[k, :, lanes_of(t, wd)].astype(F32)


def clear_edges(dst):
    tiles, count, span = dst.shape[:3]
    edge = jnp.zeros((tiles, count, 8, LANES), F32)
    dst[:, :, 0:8, :] = edge
    dst[:, :, span - 8 : span, :] = edge


def own_kernel(
    vis_in, cot_in, kernel_in, band, taps, part, mask_out, vis, cot, kernel, sems
):
    copies = fetch((cot_in, kernel_in, vis_in), (cot, kernel, vis), sems)
    height, width, chans = cot.shape
    copies[2].wait()
    mask = column_mask(vis, width)
    mask_out[...] = mask
    tiles = tiles_of(chans)
    clear_edges(band)
    copies[1].wait()
    for t, wd in tiles:
        taps[t, :, :, 0:wd] = jnp.broadcast_to(
            kernel[:, lanes_of(t, wd)][:, None, :], (KS * KS, 8, wd)
        )
        if wd < LANES:
            taps[t, :, :, wd:LANES] = jnp.zeros((KS * KS, 8, LANES - wd), F32)
    copies[0].wait()
    for t, wd in tiles:
        for k in range(height):
            if wd < LANES:
                band[t, k, 8 : 8 + width, wd:LANES] = jnp.zeros((width, LANES - wd), F32)
            band[t, k, 8 : 8 + width, 0:wd] = cot[k, :, lanes_of(t, wd)].astype(F32) * mask[:, :wd]
    half = width // 2

    def step(u, carry):
        t, h = u // 2, (u % 2) * half
        acc = [jnp.zeros((half // 8, 8, LANES), F32) for _ in range(height)]
        for s in range(height):
            for j in range(KS):
                value = band[t, s, pl.ds(h + 5 + j, half), :].reshape(half // 8, 8, LANES)
                for p in range(height):
                    i = s + 3 - p
                    acc[p] = acc[p] + value * taps[t, 48 - (KS * i + j)][None]
        for p in range(height):
            part[t, p, pl.ds(pl.multiple_of(h, 8), half), :] = acc[p].reshape(half, LANES)
        return carry

    lax.fori_loop(0, 2 * len(tiles), step, 0)


def back_kernel(before, after, band, taps, part, mask, pre, halo, total):
    height, width = part.shape[1:3]
    chans = pre.shape[1]
    tiles = tiles_of(chans)
    clear_edges(halo)
    fill_band(halo, 0, before, tiles)
    fill_band(halo, 3, after, tiles)
    half = width // 2

    def step(u, carry):
        t, h = u // 2, (u % 2) * half
        here = pl.ds(pl.multiple_of(h, 8), half)
        acc = [part[t, p, here, :].reshape(half // 8, 8, LANES) for p in range(height)]
        for m in range(6):
            s = m if m < 3 else m + height
            for j in range(KS):
                value = halo[t, m, pl.ds(h + 5 + j, half), :].reshape(half // 8, 8, LANES)
                for p in range(height):
                    i = s - p
                    if 0 <= i < KS:
                        acc[p] = acc[p] + value * taps[t, 48 - (KS * i + j)][None]
        keep = mask[here, :]
        lanes = pl.ds(pl.multiple_of(t * LANES, LANES), LANES)
        for p in range(height):
            own = band[t, p, pl.ds(pl.multiple_of(h + 8, 8), half), :]
            value = own + keep * acc[p].reshape(half, LANES)
            total[pl.ds(pl.multiple_of(p * width + h, 8), half), lanes] = value
        return carry

    lax.fori_loop(0, 2 * len(tiles), step, 0)
    pre[...] = total[:, :chans].astype(BF16)

def product_kernel(place, patches, pre, c0, c1, c2, c3, prod):
    chunks = (c0, c1, c2, c3)
    scale = 1.0 / math.sqrt(pre.shape[0] * 16)
    depth = patches.shape[0] // 4
    share = depth // 4
    for k in range(4):
        prod[...] = scale * jnp.dot(
            patches[k * depth : (k + 1) * depth, :], pre[...], preferred_element_type=F32
        )
        for d in range(4):
            to = lax.rem(place[0] + d, 4)
            at = pl.ds(pl.multiple_of(to * share, 8), share)
            chunks[d][k] = prod[at, :].astype(BF16)


def grad_kernel(down, cots, halo, grads, band, kg):
    height, width, chans = down.shape
    tiles = tiles_of(chans)
    clear_edges(band)
    fill_band(band, 0, down, tiles)
    half = width // 2

    def step(u, carry):
        t, h = u // 2, (u % 2) * half
        here = pl.ds(pl.multiple_of(h + 8, 8), half)
        mine = [halo[t, m, here, :] for m in range(3)]
        mine += [cots[t, p, here, :] for p in range(height)]
        mine += [halo[t, m, here, :] for m in range(3, 6)]
        mine = [m.reshape(half // 8, 8, LANES) for m in mine]
        for j in range(KS):
            part = [jnp.zeros((8, LANES), F32) for _ in range(KS)]
            for r in range(height):
                value = band[t, r, pl.ds(h + 5 + j, half), :].reshape(half // 8, 8, LANES)
                for i in range(KS):
                    part[i] = part[i] + jnp.sum(value * mine[r + 6 - i], axis=0)
            for i in range(KS):
                kg[u, KS * i + j] = part[i]
        kg[u, KS * KS] = sum(jnp.sum(m, axis=0) for m in mine[3 : 3 + height])
        return carry

    lax.fori_loop(0, 2 * len(tiles), step, 0)
    scale = 1.0 / math.sqrt(height * 16 * width)
    for t, wd in tiles:
        term = jnp.sum(kg[2 * t] + kg[2 * t + 1], axis=1) * scale
        grads[0 : KS * KS + 1, lanes_of(t, wd)] = term[:, :wd]


def front_kernel(down, before, after, taps, bias, mask, features, outs, band):
    height, width, chans = features.shape
    tiles = tiles_of(chans)
    clear_edges(band)
    fill_band(band, 0, before, tiles)
    fill_band(band, 3, down, tiles)
    fill_band(band, 3 + height, after, tiles)
    half = width // 2

    def step(u, carry):
        t, h = u // 2, (u % 2) * half
        acc = [jnp.zeros((half // 8, 8, LANES), F32) for _ in range(height)]
        for s in range(height + 6):
            for j in range(KS):
                value = band[t, s, pl.ds(h + 5 + j, half), :].reshape(half // 8, 8, LANES)
                for p in range(height):
                    i = s - p
                    if 0 <= i < KS:
                        acc[p] = acc[p] + value * taps[t, KS * i + j][None]
        for p in range(height):
            outs[t, p, pl.ds(pl.multiple_of(h, 8), half), :] = acc[p].reshape(half, LANES)
        return carry

    lax.fori_loop(0, 2 * len(tiles), step, 0)
    for t, wd in tiles:
        lanes = lanes_of(t, wd)
        for p in range(height):
            value = (outs[t, p, :, 0:wd] + bias[lanes][None]) * mask[:, :wd]
            own = band[t, 3 + p, 8 : 8 + width, 0:wd]
            features[p, :, lanes] = (own + value).astype(BF16)


def image_kernel(
    pre, weight, normed, rstd, gain, grads, image_grad, small, column, sort, flat, sums
):
    rows, chans, cols = image_grad.shape
    height, width = rows // 2, cols // 2
    scale = 1.0 / math.sqrt(height * 16 * width)
    gain_column(gain, column)
    sort[...] = sorter(width, True)
    value = jnp.dot(pre[...], weight[...], preferred_element_type=F32)
    flat[...] = jnp.transpose(value)
    gain_sum = jnp.zeros((chans, LANES), F32)
    for a in range(2):
        for pair in range(height // 2):
            top = 4 * pair + a
            lanes = lanes_of(pair, LANES)
            two = []
            for b in range(2):
                k = 2 * a + b
                here = slice(k * chans, (k + 1) * chans)
                value = flat[here, lanes]
                norm = normed[here, lanes].astype(F32)
                gain_sum = gain_sum + norm * value
                g = value * column[...]
                mean_g = jnp.sum(g, axis=0, keepdims=True) * (1.0 / chans)
                mean_n = jnp.sum(g * norm, axis=0, keepdims=True) * (1.0 / chans)
                g = (g - mean_g - norm * mean_n) * rstd[k : k + 1, lanes]
                two.append(g.astype(BF16))
            out = jnp.dot(jnp.concatenate(two, axis=1), sort[...], preferred_element_type=F32)
            image_grad[top] = out[:, :cols].astype(BF16)
            image_grad[top + 2] = out[:, cols:].astype(BF16)
    ones = jnp.ones((8, pre.shape[0]), BF16)
    gain_row = jnp.sum(jnp.transpose(gain_sum), axis=0, keepdims=True)
    taps = KS * KS + 1
    sums[...] = jnp.zeros(sums.shape, F32)
    sums[0:taps, :] = grads[0:taps, :]
    bias_sum = jnp.dot(ones, pre[...], preferred_element_type=F32)[0:1]
    sums[taps : taps + 1, :] = bias_sum * scale
    sums[taps + 1 : taps + 2, 0:chans] = gain_row * scale
    small[...] = sums[...].astype(BF16)


def middle_kernel(place, c0, c1, c2, c3, *outs):
    for k in (1, 2, 3):
        to = jnp.bitwise_xor(place[0], k)
        outs[k - 1][...] = sum_four(c0[to], c1[to], c2[to], c3[to]).astype(BF16)


def last_kernel(
    place, c0, c1, c2, c3, w2, w3, w1, t0, t1, t2, t3,
    weight, gain, bias, kernel, depth_bias,
):
    z = place[0]
    own = sum_four(c0[z], c1[z], c2[z], c3[z])
    weight[...] = sum_four(own, w1[...], w2[...], w3[...])
    total = sum_four(t0[...], t1[...], t2[...], t3[...])
    taps = KS * KS
    kernel[...] = total[:taps]
    depth_bias[...] = total[taps]
    bias[...] = total[taps + 1]
    gain[...] = total[taps + 2, : gain.shape[0]]


def sd(shape, dtype):
    return jax.ShapeDtypeStruct(shape, dtype)


def sum_four(own, one, two, three):
    return (own.astype(F32) + two.astype(F32)) + (one.astype(F32) + three.astype(F32))


def send(values, pairs):
    return [lax.ppermute(value, "rows", pair) for value, pair in zip(values, pairs)]


def body(image, visible, layer_norm_gain, reducer_weight, reducer_bias, depth_kernel, depth_bias, cotangent):
    height, width, chans = cotangent.shape
    rows, cols, in_chans = image.shape
    image = jnp.transpose(image, (0, 2, 1))
    weight = jnp.transpose(reducer_weight)
    pixels = height * width
    bands = lax.axis_size("rows")
    index = lax.axis_index("rows")
    place_y = (index % 4).reshape(1).astype(jnp.int32)
    place_z = (index // 4).reshape(1).astype(jnp.int32)
    up = [(i, i + 1) for i in range(bands - 1)]
    low = [(j, i) for i, j in up]
    ring = [(z, y) for z in range(4) for y in range(4)]
    along_y = [[(4 * z + y, 4 * z + (y + k) % 4) for z, y in ring] for k in (1, 2, 3)]
    along_z = [[(4 * z + y, 4 * (z ^ k) + y) for z, y in ring] for k in (1, 2, 3)]
    tiles = len(tiles_of(chans))
    share = in_chans // 4
    halo = sd((3, width, chans), BF16)
    span = width + 16

    column = pltpu.VMEM((in_chans, LANES), F32)
    sort = pltpu.VMEM((4 * width, 4 * width), BF16)
    cot_first, cot_last, patches, normed, rstd, down, down_first, down_last = call(
        reduce_kernel,
        (
            halo,
            halo,
            sd((4 * in_chans, pixels), BF16),
            sd((4 * in_chans, pixels), BF16),
            sd((8, pixels), F32),
            sd((height, width, chans), BF16),
            halo,
            halo,
        ),
        [HBM] * 6,
        [
            column,
            sort,
            pltpu.SMEM((1, width // PATCH), jnp.int32),
            pltpu.VMEM((height, width, chans), BF16),
            pltpu.VMEM(image.shape, BF16),
            pltpu.VMEM((in_chans,), F32),
            pltpu.VMEM(weight.shape, BF16),
            pltpu.VMEM((chans,), F32),
            pltpu.SemaphoreType.DMA((6,)),
        ],
        "reduce",
        60,
        2 * 10**7,
    )(visible, cotangent, image, layer_norm_gain, weight, reducer_bias)
    cot_before = lax.ppermute(cot_last, "rows", up)
    cot_after = lax.ppermute(cot_first, "rows", low)
    down_before = lax.ppermute(down_last, "rows", up)
    down_after = lax.ppermute(down_first, "rows", low)

    vis_own, _ = lax.optimization_barrier((visible, rstd))
    band, taps, part, mask = call(
        own_kernel,
        (
            sd((tiles, height, span, LANES), F32),
            sd((tiles, KS * KS, 8, LANES), F32),
            sd((tiles, height, width, LANES), F32),
            sd((width, LANES), F32),
        ),
        [HBM] * 3,
        [
            pltpu.SMEM((1, width // PATCH), jnp.int32),
            pltpu.VMEM((height, width, chans), BF16),
            pltpu.VMEM((KS * KS, chans), F32),
            pltpu.SemaphoreType.DMA((3,)),
        ],
        "own",
        16,
        5 * 10**7,
    )(vis_own, cotangent, depth_kernel)

    pre, halo_rows = call(
        back_kernel,
        (sd((pixels, chans), BF16), sd((tiles, 6, span, LANES), F32)),
        [VM] * 6,
        [pltpu.VMEM((pixels, tiles * LANES), F32)],
        "back",
        16,
        10**9,
    )(cot_before, cot_after, band, taps, part, mask)
    chunks = call(
        product_kernel,
        [sd((4, share, chans), BF16)] * 4,
        [SM] + [VM] * 2,
        [pltpu.VMEM((in_chans, chans), F32)],
        "product",
    )(place_y, patches, pre)
    got = send(chunks[1:], along_y)
    down, down_before, down_after = lax.optimization_barrier((down, down_before, down_after))

    grads = call(
        grad_kernel,
        sd((56, chans), F32),
        [VM] * 3,
        [
            pltpu.VMEM((tiles, height, span, LANES), F32),
            pltpu.VMEM((2 * tiles, KS * KS + 1, 8, LANES), F32),
        ],
        "grads",
    )(down, band, halo_rows)
    image_grad, small = call(
        image_kernel,
        (sd((rows, in_chans, cols), BF16), sd((56, chans), BF16)),
        [VM] * 6,
        [column, sort, pltpu.VMEM((4 * in_chans, pixels), F32), pltpu.VMEM((56, chans), F32)],
        "image",
    )(pre, weight, normed, rstd, layer_norm_gain, grads)
    image_grad = jnp.transpose(image_grad, (0, 2, 1))
    got_t = send([small] * 3, along_z)
    parts = call(
        middle_kernel,
        (sd((share, chans), BF16),) * 3,
        [SM] + [VM] * 4,
        [],
        "middle",
        16,
        4 * 10**7,
    )(place_z, chunks[0], *got)
    got_w = send([parts[k] for k in (1, 2, 0)], [along_z[k] for k in (1, 2, 0)])
    front_mask, _ = lax.optimization_barrier((mask, parts[0]))
    features = call(
        front_kernel,
        sd((height, width, chans), BF16),
        [VM] * 6,
        [
            pltpu.VMEM((tiles, height, width, LANES), F32),
            pltpu.VMEM((tiles, height + 6, span, LANES), F32),
        ],
        "front",
        16,
        10**7,
    )(down, down_before, down_after, taps, depth_bias, front_mask)
    small = sum_four(small, *got_t).astype(BF16)
    got_t = send([small] * 3, along_y)
    down_weight_grad, gain_grad, bias_grad, kernel_grad, depth_bias_grad = call(
        last_kernel,
        (
            sd((share, chans), F32),
            sd((in_chans,), F32),
            sd((chans,), F32),
            sd((KS * KS, chans), F32),
            sd((chans,), F32),
        ),
        [SM] + [VM] * 11,
        [],
        "last",
    )(place_z, chunks[0], *got, *got_w, small, *got_t)
    return (
        features,
        image_grad,
        down_weight_grad,
        gain_grad,
        bias_grad,
        kernel_grad,
        depth_bias_grad,
    )


def solution(mesh):
    placed = (
        P(("group", "rows"), None, None),
        P(("group", "rows"), None),
        P(),
        P(),
        P(),
        P(),
        P(),
        P(("group", "rows"), None, None),
    )
    return jax.shard_map(
        body,
        mesh=mesh,
        in_specs=placed,
        out_specs=(
            P(("group", "rows"), None, None),
            P(("group", "rows"), None, None),
            P(("group", "rows"), None),
            P("group"),
            P("group"),
            P("group", None),
            P("group"),
        ),
        check_vma=False,
    )
```

```python
import math

import jax
import jax.numpy as jnp
from jax import lax
from jax.experimental import pallas as pl
from jax.experimental.pallas import tpu as pltpu
from jax.sharding import PartitionSpec as P

KS = 7
PATCH = 4
LANES = 128
F32 = jnp.float32
BF16 = jnp.bfloat16
VM = pl.BlockSpec(memory_space=pltpu.VMEM)
SM = pl.BlockSpec(memory_space=pltpu.SMEM)
HBM = pl.BlockSpec(memory_space=pltpu.HBM)


def tiles_of(chans):
    return [(t, min(LANES, chans - t * LANES)) for t in range(-(-chans // LANES))]


def lanes_of(t, wd):
    return slice(t * LANES, t * LANES + wd)


def column_mask(vis, width):
    row = lax.broadcasted_iota(jnp.int32, (width, LANES), 0) // PATCH
    mask = jnp.zeros((width, LANES), F32)
    for k in range(width // PATCH):
        mask = jnp.where(row == k, vis[0, k].astype(F32), mask)
    return mask


def fetch(sources, targets, sems):
    copies = [
        pltpu.make_async_copy(source, target, sems.at[k])
        for k, (source, target) in enumerate(zip(sources, targets))
    ]
    for copy in copies:
        copy.start()
    return copies


def call(kernel, out_shape, in_specs, scratch, name, vmem=16, size=10**5):
    return pl.pallas_call(
        kernel,
        out_shape=out_shape,
        in_specs=in_specs,
        out_specs=jax.tree.map(lambda _: VM, out_shape),
        scratch_shapes=scratch,
        compiler_params=pltpu.CompilerParams(vmem_limit_bytes=vmem * 2**20),
        cost_estimate=pl.CostEstimate(flops=10**6, bytes_accessed=size, transcendentals=0),
        name=name,
    )


def sorter(width, back):
    size = 4 * width
    row = lax.broadcasted_iota(jnp.int32, (size, size), 1 if back else 0)
    col = lax.broadcasted_iota(jnp.int32, (size, size), 0 if back else 1)
    half, rest = col // (2 * width), col % (2 * width)
    source = (rest // width) * (2 * width) + 2 * (rest % width) + half
    return jnp.where(row == source, 1.0, 0.0).astype(BF16)


def gain_column(gain, column):
    column[...] = jnp.transpose(jnp.broadcast_to(gain[...][None], (LANES, gain.shape[0])))


def reduce_kernel(
    vis_in, cot_in, image_in, gain_in, weight_in, bias_in,
    cot_first, cot_last, patches, normed, rstd, down, first, last,
    column, sort, vis, cot, image, gain, weight, bias, sems,
):
    copies = fetch(
        (image_in, gain_in, weight_in, bias_in, vis_in, cot_in),
        (image, gain, weight, bias, vis, cot),
        sems,
    )
    rows, chans, cols = image.shape
    height, width = rows // 2, cols // 2
    copies[4].wait()
    mask = column_mask(vis, width)
    copies[5].wait()
    for t, wd in tiles_of(cot.shape[2]):
        lanes = lanes_of(t, wd)
        for p in range(height):
            row = (cot[p, :, lanes].astype(F32) * mask[:, :wd]).astype(BF16)
            if p < 3:
                cot_first[p, :, lanes] = row
            if p >= height - 3:
                cot_last[p - (height - 3), :, lanes] = row
    sort[...] = sorter(width, False)
    copies[1].wait()
    gain_column(gain, column)
    copies[0].wait()
    for a in range(2):
        for pair in range(height // 2):
            top = 4 * pair + a
            two = jnp.concatenate([image[top], image[top + 2]], axis=1)
            x = jnp.dot(two, sort[...], preferred_element_type=F32)
            center = jnp.sum(x, axis=0, keepdims=True) * (1.0 / chans)
            x = x - center
            var = jnp.sum(x * x, axis=0, keepdims=True) * (1.0 / chans)
            inv = 1.0 / jnp.sqrt(var + 1e-06)
            x = x * inv
            lanes = lanes_of(pair, LANES)
            for b in range(2):
                k = 2 * a + b
                here = slice(k * chans, (k + 1) * chans)
                part = x[:, lanes_of(b, LANES)]
                normed[here, lanes] = part.astype(BF16)
                patches[here, lanes] = (part * column[...]).astype(BF16)
                rstd[k : k + 1, lanes] = inv[:, lanes_of(b, LANES)]
    copies[2].wait()
    copies[3].wait()
    acc = jnp.dot(weight[...], patches[...], preferred_element_type=F32)
    acc = jnp.transpose(acc) + bias[...][None]
    for t, wd in tiles_of(weight.shape[0]):
        lanes = lanes_of(t, wd)
        for p in range(height):
            row = (acc[p * width : (p + 1) * width, lanes] * mask[:, :wd]).astype(BF16)
            down[p, :, lanes] = row
            if p < 3:
                first[p, :, lanes] = row
            if p >= height - 3:
                last[p - (height - 3), :, lanes] = row


def fill_band(dst, at, ref, tiles):
    count, width = ref.shape[:2]
    for t, wd in tiles:
        for k in range(count):
            if wd < LANES:
                dst[t, at + k, 8 : 8 + width, wd:LANES] = jnp.zeros((width, LANES - wd), F32)
            dst[t, at + k, 8 : 8 + width, 0:wd] = ref[k, :, lanes_of(t, wd)].astype(F32)


def clear_edges(dst):
    tiles, count, span = dst.shape[:3]
    edge = jnp.zeros((tiles, count, 8, LANES), F32)
    dst[:, :, 0:8, :] = edge
    dst[:, :, span - 8 : span, :] = edge


def own_kernel(
    vis_in, cot_in, kernel_in, band, taps, part, mask_out, vis, cot, kernel, sems
):
    copies = fetch((cot_in, kernel_in, vis_in), (cot, kernel, vis), sems)
    height, width, chans = cot.shape
    copies[2].wait()
    mask = column_mask(vis, width)
    mask_out[...] = mask
    tiles = tiles_of(chans)
    clear_edges(band)
    copies[1].wait()
    for t, wd in tiles:
        taps[t, :, :, 0:wd] = jnp.broadcast_to(
            kernel[:, lanes_of(t, wd)][:, None, :], (KS * KS, 8, wd)
        )
        if wd < LANES:
            taps[t, :, :, wd:LANES] = jnp.zeros((KS * KS, 8, LANES - wd), F32)
    copies[0].wait()
    for t, wd in tiles:
        for k in range(height):
            if wd < LANES:
                band[t, k, 8 : 8 + width, wd:LANES] = jnp.zeros((width, LANES - wd), F32)
            band[t, k, 8 : 8 + width, 0:wd] = cot[k, :, lanes_of(t, wd)].astype(F32) * mask[:, :wd]
    half = width // 2

    def step(u, carry):
        t, h = u // 2, (u % 2) * half
        acc = [jnp.zeros((half // 8, 8, LANES), F32) for _ in range(height)]
        for s in range(height):
            for j in range(KS):
                value = band[t, s, pl.ds(h + 5 + j, half), :].reshape(half // 8, 8, LANES)
                for p in range(height):
                    i = s + 3 - p
                    acc[p] = acc[p] + value * taps[t, 48 - (KS * i + j)][None]
        for p in range(height):
            part[t, p, pl.ds(pl.multiple_of(h, 8), half), :] = acc[p].reshape(half, LANES)
        return carry

    lax.fori_loop(0, 2 * len(tiles), step, 0)


def back_kernel(before, after, band, taps, part, mask, pre, halo, total):
    height, width = part.shape[1:3]
    chans = pre.shape[1]
    tiles = tiles_of(chans)
    clear_edges(halo)
    fill_band(halo, 0, before, tiles)
    fill_band(halo, 3, after, tiles)
    half = width // 2

    def step(u, carry):
        t, h = u // 2, (u % 2) * half
        here = pl.ds(pl.multiple_of(h, 8), half)
        acc = [part[t, p, here, :].reshape(half // 8, 8, LANES) for p in range(height)]
        for m in range(6):
            s = m if m < 3 else m + height
            for j in range(KS):
                value = halo[t, m, pl.ds(h + 5 + j, half), :].reshape(half // 8, 8, LANES)
                for p in range(height):
                    i = s - p
                    if 0 <= i < KS:
                        acc[p] = acc[p] + value * taps[t, 48 - (KS * i + j)][None]
        keep = mask[here, :]
        lanes = pl.ds(pl.multiple_of(t * LANES, LANES), LANES)
        for p in range(height):
            own = band[t, p, pl.ds(pl.multiple_of(h + 8, 8), half), :]
            value = own + keep * acc[p].reshape(half, LANES)
            total[pl.ds(pl.multiple_of(p * width + h, 8), half), lanes] = value
        return carry

    lax.fori_loop(0, 2 * len(tiles), step, 0)
    pre[...] = total[:, :chans].astype(BF16)

def product_kernel(place, patches, pre, c0, c1, c2, c3, prod):
    chunks = (c0, c1, c2, c3)
    scale = 1.0 / math.sqrt(pre.shape[0] * 16)
    depth = patches.shape[0] // 4
    share = depth // 4
    for k in range(4):
        prod[...] = scale * jnp.dot(
            patches[k * depth : (k + 1) * depth, :], pre[...], preferred_element_type=F32
        )
        for d in range(4):
            to = lax.rem(place[0] + d, 4)
            at = pl.ds(pl.multiple_of(to * share, 8), share)
            chunks[d][k] = prod[at, :].astype(BF16)


def grad_kernel(down, cots, halo, grads, band, kg):
    height, width, chans = down.shape
    tiles = tiles_of(chans)
    clear_edges(band)
    fill_band(band, 0, down, tiles)
    half = width // 2

    def step(u, carry):
        t, h = u // 2, (u % 2) * half
        here = pl.ds(pl.multiple_of(h + 8, 8), half)
        mine = [halo[t, m, here, :] for m in range(3)]
        mine += [cots[t, p, here, :] for p in range(height)]
        mine += [halo[t, m, here, :] for m in range(3, 6)]
        mine = [m.reshape(half // 8, 8, LANES) for m in mine]
        for j in range(KS):
            part = [jnp.zeros((8, LANES), F32) for _ in range(KS)]
            for r in range(height):
                value = band[t, r, pl.ds(h + 5 + j, half), :].reshape(half // 8, 8, LANES)
                for i in range(KS):
                    part[i] = part[i] + jnp.sum(value * mine[r + 6 - i], axis=0)
            for i in range(KS):
                kg[u, KS * i + j] = part[i]
        kg[u, KS * KS] = sum(jnp.sum(m, axis=0) for m in mine[3 : 3 + height])
        return carry

    lax.fori_loop(0, 2 * len(tiles), step, 0)
    scale = 1.0 / math.sqrt(height * 16 * width)
    for t, wd in tiles:
        term = jnp.sum(kg[2 * t] + kg[2 * t + 1], axis=1) * scale
        grads[0 : KS * KS + 1, lanes_of(t, wd)] = term[:, :wd]


def front_kernel(down, before, after, taps, bias, mask, features, outs, band):
    height, width, chans = features.shape
    tiles = tiles_of(chans)
    clear_edges(band)
    fill_band(band, 0, before, tiles)
    fill_band(band, 3, down, tiles)
    fill_band(band, 3 + height, after, tiles)
    half = width // 2

    def step(u, carry):
        t, h = u // 2, (u % 2) * half
        acc = [jnp.zeros((half // 8, 8, LANES), F32) for _ in range(height)]
        for s in range(height + 6):
            for j in range(KS):
                value = band[t, s, pl.ds(h + 5 + j, half), :].reshape(half // 8, 8, LANES)
                for p in range(height):
                    i = s - p
                    if 0 <= i < KS:
                        acc[p] = acc[p] + value * taps[t, KS * i + j][None]
        for p in range(height):
            outs[t, p, pl.ds(pl.multiple_of(h, 8), half), :] = acc[p].reshape(half, LANES)
        return carry

    lax.fori_loop(0, 2 * len(tiles), step, 0)
    for t, wd in tiles:
        lanes = lanes_of(t, wd)
        for p in range(height):
            value = (outs[t, p, :, 0:wd] + bias[lanes][None]) * mask[:, :wd]
            own = band[t, 3 + p, 8 : 8 + width, 0:wd]
            features[p, :, lanes] = (own + value).astype(BF16)


def image_kernel(
    pre, weight, normed, rstd, gain, grads, image_grad, small, column, sort, flat, sums
):
    rows, chans, cols = image_grad.shape
    height, width = rows // 2, cols // 2
    scale = 1.0 / math.sqrt(height * 16 * width)
    gain_column(gain, column)
    sort[...] = sorter(width, True)
    value = jnp.dot(pre[...], weight[...], preferred_element_type=F32)
    flat[...] = jnp.transpose(value)
    gain_sum = jnp.zeros((chans, LANES), F32)
    for a in range(2):
        for pair in range(height // 2):
            top = 4 * pair + a
            lanes = lanes_of(pair, LANES)
            two = []
            for b in range(2):
                k = 2 * a + b
                here = slice(k * chans, (k + 1) * chans)
                value = flat[here, lanes]
                norm = normed[here, lanes].astype(F32)
                gain_sum = gain_sum + norm * value
                g = value * column[...]
                mean_g = jnp.sum(g, axis=0, keepdims=True) * (1.0 / chans)
                mean_n = jnp.sum(g * norm, axis=0, keepdims=True) * (1.0 / chans)
                g = (g - mean_g - norm * mean_n) * rstd[k : k + 1, lanes]
                two.append(g.astype(BF16))
            out = jnp.dot(jnp.concatenate(two, axis=1), sort[...], preferred_element_type=F32)
            image_grad[top] = out[:, :cols].astype(BF16)
            image_grad[top + 2] = out[:, cols:].astype(BF16)
    ones = jnp.ones((8, pre.shape[0]), BF16)
    gain_row = jnp.sum(jnp.transpose(gain_sum), axis=0, keepdims=True)
    taps = KS * KS + 1
    sums[...] = jnp.zeros(sums.shape, F32)
    sums[0:taps, :] = grads[0:taps, :]
    bias_sum = jnp.dot(ones, pre[...], preferred_element_type=F32)[0:1]
    sums[taps : taps + 1, :] = bias_sum * scale
    sums[taps + 1 : taps + 2, 0:chans] = gain_row * scale
    small[...] = sums[...].astype(BF16)


def middle_kernel(place, c0, c2, c1, c3, *outs):
    for k in (1, 2, 3):
        to = jnp.bitwise_xor(place[0], k)
        outs[k - 1][...] = sum_four(c0[to], c1[to], c2[to], c3[to]).astype(BF16)


def last_kernel(
    place, c0, c2, c1, c3, w2, w3, w1, t0, t1, t2, t3,
    weight, gain, bias, kernel, depth_bias,
):
    z = place[0]
    own = sum_four(c0[z], c1[z], c2[z], c3[z])
    weight[...] = sum_four(own, w1[...], w2[...], w3[...])
    total = sum_four(t0[...], t1[...], t2[...], t3[...])
    taps = KS * KS
    kernel[...] = total[:taps]
    depth_bias[...] = total[taps]
    bias[...] = total[taps + 1]
    gain[...] = total[taps + 2, : gain.shape[0]]


def sd(shape, dtype):
    return jax.ShapeDtypeStruct(shape, dtype)


def sum_four(own, one, two, three):
    return (own.astype(F32) + two.astype(F32)) + (one.astype(F32) + three.astype(F32))


def send(values, pairs):
    return [lax.ppermute(value, "rows", pair) for value, pair in zip(values, pairs)]


def body(image, visible, layer_norm_gain, reducer_weight, reducer_bias, depth_kernel, depth_bias, cotangent):
    height, width, chans = cotangent.shape
    rows, cols, in_chans = image.shape
    image = jnp.transpose(image, (0, 2, 1))
    weight = jnp.transpose(reducer_weight)
    pixels = height * width
    bands = lax.axis_size("rows")
    index = lax.axis_index("rows")
    place_y = (index % 4).reshape(1).astype(jnp.int32)
    place_z = (index // 4).reshape(1).astype(jnp.int32)
    up = [(i, i + 1) for i in range(bands - 1)]
    low = [(j, i) for i, j in up]
    ring = [(z, y) for z in range(4) for y in range(4)]
    along_y = [[(4 * z + y, 4 * z + (y + k) % 4) for z, y in ring] for k in (1, 2, 3)]
    along_z = [[(4 * z + y, 4 * (z ^ k) + y) for z, y in ring] for k in (1, 2, 3)]
    tiles = len(tiles_of(chans))
    share = in_chans // 4
    halo = sd((3, width, chans), BF16)
    span = width + 16

    column = pltpu.VMEM((in_chans, LANES), F32)
    sort = pltpu.VMEM((4 * width, 4 * width), BF16)
    cot_first, cot_last, patches, normed, rstd, down, down_first, down_last = call(
        reduce_kernel,
        (
            halo,
            halo,
            sd((4 * in_chans, pixels), BF16),
            sd((4 * in_chans, pixels), BF16),
            sd((8, pixels), F32),
            sd((height, width, chans), BF16),
            halo,
            halo,
        ),
        [HBM] * 6,
        [
            column,
            sort,
            pltpu.SMEM((1, width // PATCH), jnp.int32),
            pltpu.VMEM((height, width, chans), BF16),
            pltpu.VMEM(image.shape, BF16),
            pltpu.VMEM((in_chans,), F32),
            pltpu.VMEM(weight.shape, BF16),
            pltpu.VMEM((chans,), F32),
            pltpu.SemaphoreType.DMA((6,)),
        ],
        "reduce",
        60,
        2 * 10**7,
    )(visible, cotangent, image, layer_norm_gain, weight, reducer_bias)
    cot_before = lax.ppermute(cot_last, "rows", up)
    cot_after = lax.ppermute(cot_first, "rows", low)
    down_before = lax.ppermute(down_last, "rows", up)
    down_after = lax.ppermute(down_first, "rows", low)

    vis_own, _ = lax.optimization_barrier((visible, rstd))
    band, taps, part, mask = call(
        own_kernel,
        (
            sd((tiles, height, span, LANES), F32),
            sd((tiles, KS * KS, 8, LANES), F32),
            sd((tiles, height, width, LANES), F32),
            sd((width, LANES), F32),
        ),
        [HBM] * 3,
        [
            pltpu.SMEM((1, width // PATCH), jnp.int32),
            pltpu.VMEM((height, width, chans), BF16),
            pltpu.VMEM((KS * KS, chans), F32),
            pltpu.SemaphoreType.DMA((3,)),
        ],
        "own",
        16,
        5 * 10**7,
    )(vis_own, cotangent, depth_kernel)

    pre, halo_rows = call(
        back_kernel,
        (sd((pixels, chans), BF16), sd((tiles, 6, span, LANES), F32)),
        [VM] * 6,
        [pltpu.VMEM((pixels, tiles * LANES), F32)],
        "back",
        16,
        10**9,
    )(cot_before, cot_after, band, taps, part, mask)
    chunks = call(
        product_kernel,
        [sd((4, share, chans), BF16)] * 4,
        [SM] + [VM] * 2,
        [pltpu.VMEM((in_chans, chans), F32)],
        "product",
    )(place_y, patches, pre)
    got = send([chunks[k] for k in (2, 1, 3)], [along_y[k - 1] for k in (2, 1, 3)])
    down, down_before, down_after = lax.optimization_barrier((down, down_before, down_after))

    grads = call(
        grad_kernel,
        sd((56, chans), F32),
        [VM] * 3,
        [
            pltpu.VMEM((tiles, height, span, LANES), F32),
            pltpu.VMEM((2 * tiles, KS * KS + 1, 8, LANES), F32),
        ],
        "grads",
    )(down, band, halo_rows)
    image_grad, small = call(
        image_kernel,
        (sd((rows, in_chans, cols), BF16), sd((56, chans), BF16)),
        [VM] * 6,
        [column, sort, pltpu.VMEM((4 * in_chans, pixels), F32), pltpu.VMEM((56, chans), F32)],
        "image",
    )(pre, weight, normed, rstd, layer_norm_gain, grads)
    image_grad = jnp.transpose(image_grad, (0, 2, 1))
    got_t = send([small] * 3, along_z)
    parts = call(
        middle_kernel,
        (sd((share, chans), BF16),) * 3,
        [SM] + [VM] * 4,
        [],
        "middle",
        16,
        4 * 10**7,
    )(place_z, chunks[0], *got)
    got_w = send([parts[k] for k in (1, 2, 0)], [along_z[k] for k in (1, 2, 0)])
    front_mask, _ = lax.optimization_barrier((mask, parts[0]))
    features = call(
        front_kernel,
        sd((height, width, chans), BF16),
        [VM] * 6,
        [
            pltpu.VMEM((tiles, height, width, LANES), F32),
            pltpu.VMEM((tiles, height + 6, span, LANES), F32),
        ],
        "front",
        16,
        10**7,
    )(down, down_before, down_after, taps, depth_bias, front_mask)
    small = sum_four(small, *got_t).astype(BF16)
    got_t = send([small] * 3, along_y)
    down_weight_grad, gain_grad, bias_grad, kernel_grad, depth_bias_grad = call(
        last_kernel,
        (
            sd((share, chans), F32),
            sd((in_chans,), F32),
            sd((chans,), F32),
            sd((KS * KS, chans), F32),
            sd((chans,), F32),
        ),
        [SM] + [VM] * 11,
        [],
        "last",
    )(place_z, chunks[0], *got, *got_w, small, *got_t)
    return (
        features,
        image_grad,
        down_weight_grad,
        gain_grad,
        bias_grad,
        kernel_grad,
        depth_bias_grad,
    )


def solution(mesh):
    placed = (
        P(("group", "rows"), None, None),
        P(("group", "rows"), None),
        P(),
        P(),
        P(),
        P(),
        P(),
        P(("group", "rows"), None, None),
    )
    return jax.shard_map(
        body,
        mesh=mesh,
        in_specs=placed,
        out_specs=(
            P(("group", "rows"), None, None),
            P(("group", "rows"), None, None),
            P(("group", "rows"), None),
            P("group"),
            P("group"),
            P("group", None),
            P("group"),
        ),
        check_vma=False,
    )
```
